128 devices in a mesh: row: 8 (over y, x_lo), col: 16 (over x_hi, z, core).
Axes of the slice: x: 4 (x_hi: 2, x_lo: 2; x = x_hi * 2 + x_lo), y: 4, z: 4, core: 2. Of those that a mesh axis runs over, the one named last changes fastest.
Arguments:
- front: float32 [16384, 16384], P('row', 'col'), may hold values from -6 to 6
- contrib: float32 [8192, 16384], P('row', 'col'), may hold values from -6 to 6
- pivot_inverse: float32 [4, 256, 256], replicated, may hold values from -0.0234375 to 0.0234375
- index_map: int32 [2, 32], replicated, may hold values from 0 to 63, as said below
- fill_mask: int32 [64, 64], replicated, may hold values from 0 to 1, as said below
Outputs:
- factored: float32 [16384, 16384], P('row', 'col')
The draws below stay inside these ranges and needn't reach their ends.
Inputs may be any that keep to these rules, and one draw needn't show every extreme that they name: For each child h, index_map[h, a] = a + t_h(floor(a / 8)), where t_h is nondecreasing, t_h(0) <= 8 and t_h grows by at most 8 from one group to the next. For one of the two children, drawn from the seed, t_h(g) = (g + 1) * 8 for every group g. Hence every parent process row owns exactly 4 of a child's block indices, and the 4 consecutive child block columns held by one device land on distinct parent process columns. 1 marks a block of the fill pattern. It contains every block (index_map[h, a], index_map[h, b]) and is closed under the first 4 steps: for k < 4, i > k, j > k, fill_mask[i, k] = fill_mask[k, j] = 1 implies fill_mask[i, j] = 1.
All inputs are finite; a program needn't handle non-finite values.
Results may differ from the reference program's by a relative error of at most 0.00021.
Values sent between devices are 32-bit elements; how exact they have to be, the bound alone decides.
A program may use at most 192 MiB of HBM per device.

```python
import jax
import jax.numpy as jnp
from jax import lax

BS = 256
PBLK = 4
CBLK = 4
K = 4
PROWS = 8
PCOLS = 16
NB = 64
NC = 32
NBR = 8


def shared_maps(key):
    row_count = NC // CBLK
    first_shift = jax.random.randint(jax.random.fold_in(key, 11), (2, 1), 0, row_count + 1)
    steps_up = jax.random.randint(jax.random.fold_in(key, 12), (2, CBLK - 1), 0, row_count + 1)
    full_child = jax.random.randint(jax.random.fold_in(key, 13), (), 0, 2)
    is_full = (jnp.arange(2, dtype=jnp.int32) == full_child)[:, None]
    first_shift = jnp.where(is_full, row_count, first_shift)
    steps_up = jnp.where(is_full, row_count, steps_up)
    shifts = jnp.concatenate([first_shift, first_shift + jnp.cumsum(steps_up, axis=1)], axis=1)
    positions = jnp.arange(NC, dtype=jnp.int32)
    return (positions[None, :] + jnp.repeat(shifts, row_count, axis=1)).astype(jnp.int32)


def draw_index_map(key, part):
    return shared_maps(key)


def draw_fill_mask(key, part):
    block_map = shared_maps(key)
    key = jax.random.fold_in(key, 5)
    levels = jax.random.randint(jax.random.fold_in(key, 1), (1, NB), 0, 4)
    coins = jax.random.randint(jax.random.fold_in(key, 2), (NB, NB), 0, 8)
    pattern = coins < levels
    blocks_all = jnp.arange(NB, dtype=jnp.int32)
    for child_index in range(2):
        member = jnp.any(block_map[child_index][:, None] == blocks_all[None, :], axis=0)
        pattern = pattern | member[:, None] & member[None, :]
    for panel_index in range(K):
        later_blocks = blocks_all > panel_index
        grown_fill = pattern[:, panel_index][:, None] & pattern[panel_index, :][None, :]
        pattern = pattern | grown_fill & later_blocks[:, None] & later_blocks[None, :]
    return pattern.astype(jnp.int32)


def level_of(stream_key, shape, cuts, smallest, high):
    def one(axis_at, parts):
        steps = jax.random.uniform(jax.random.fold_in(jax.random.fold_in(stream_key, 6), axis_at), (parts,), jnp.float32, smallest / len(cuts), high / len(cuts))
        return jnp.repeat(jnp.exp(steps), shape[axis_at] // parts).reshape((-1,) + (1,) * (len(shape) - axis_at - 1))

    factor_of = one(*cuts[0])
    for cut in cuts[1:]:
        factor_of = factor_of * one(*cut)
    return factor_of


def noise(stream_key, extent, deviation, limit, pieces=(), held_as=jnp.bfloat16):
    array = jax.random.normal(stream_key, extent, jnp.float32) * deviation
    if len(pieces) > 0:
        array = level_of(stream_key, extent, pieces, -0.22, 0.18) * array
    return jnp.clip(array, min=-limit, max=limit).astype(held_as)


def setup_inputs(seed: int = 0) -> dict:
    keys = jax.random.split(jax.random.key(seed), 6)
    front = noise(keys[0], (NB * BS, NB * BS), 1.0, 6.0, ((0, 8), (1, 16)), jnp.float32)
    contrib = noise(keys[1], (NC * BS, 2 * NC * BS), 1.0, 6.0, ((0, 8), (1, 16)), jnp.float32)
    pivot_inverse = noise(keys[2], (K, BS, BS), (BS * BS) ** -0.5, 0.0234375, (), jnp.float32)
    index_map = draw_index_map(jax.random.fold_in(keys[5], 71), 0)
    fill_mask = draw_fill_mask(jax.random.fold_in(keys[5], 71), 0)
    return dict(front=front, contrib=contrib, pivot_inverse=pivot_inverse, index_map=index_map, fill_mask=fill_mask)


exact_mode = lax.Precision.HIGHEST


def row_store(block_index):
    return (block_index % PROWS) * NBR + block_index // PROWS


def col_store(block_index):
    return (block_index % PCOLS) * PBLK + block_index // PCOLS


def reference(front, contrib, pivot_inverse, index_map, fill_mask):
    blocks = front.reshape(NB, BS, NB, BS)
    positions = jnp.arange(NC, dtype=jnp.int32)
    for child_index in range(2):
        block_map = index_map[child_index].astype(jnp.int32)
        order_key = (block_map % PROWS) * NC + positions
        ordering = jnp.argsort(order_key).astype(jnp.int32)
        target_rows = row_store(block_map[ordering]).astype(jnp.int32)
        target_cols = col_store(block_map).astype(jnp.int32)
        child_part = contrib[:, child_index * NC * BS:(child_index + 1) * NC * BS]
        child_part = child_part.reshape(NC, BS, NC, BS).transpose(0, 2, 1, 3)
        blocks = blocks.at[target_rows[:, None], :, target_cols[None, :], :].add(child_part)
    store_index = jnp.arange(NB, dtype=jnp.int32)
    glob_rows = (store_index % NBR) * PROWS + store_index // NBR
    glob_cols = (store_index % PBLK) * PCOLS + store_index // PBLK
    store_mask = fill_mask[glob_rows[:, None], glob_cols[None, :]].astype(jnp.float32)
    matrix = (blocks * store_mask[:, None, :, None]).reshape(NB * BS, NB * BS)
    row_marks = jnp.repeat(glob_rows, BS)
    col_marks = jnp.repeat(glob_cols, BS)
    for panel_index in range(K):
        col_at = col_store(panel_index) * BS
        row_at = row_store(panel_index) * BS
        column = matrix[:, col_at:col_at + BS]
        below_rows = (row_marks > panel_index)[:, None]
        product = jnp.dot(column, pivot_inverse[panel_index], precision=exact_mode, preferred_element_type=jnp.float32)
        lower_part = jnp.where(below_rows, product, 0.0)
        upper_part = jnp.where((col_marks > panel_index)[None, :], matrix[row_at:row_at + BS, :], 0.0)
        matrix = matrix - jnp.dot(lower_part, upper_part, precision=exact_mode, preferred_element_type=jnp.float32)
        matrix = matrix.at[:, col_at:col_at + BS].set(jnp.where(below_rows, lower_part, column))
    return matrix
```

```python
import functools

import jax
import jax.numpy as jnp
from jax import lax
from jax.experimental import pallas as pl
from jax.experimental.pallas import tpu as pltpu
from jax.sharding import PartitionSpec as P

BS = 256
K = 4
MESH = pl.DeviceIdType.MESH
f32 = jnp.float32
bf16 = jnp.bfloat16


def place(imap, child, g, h, z, core):
    t = imap[child, 8 * g] - 8 * g
    first = (core + t) % 2
    start = (4 * g + (t + first) // 2) % 8
    m = (z + 8 - start) % 4
    half = ((start + m) % 8) // 4
    block = 8 * g + t + first + 2 * m
    return half == h, block // 16


def local_row(imap, child, jj, r):
    t = imap[child, 8 * jj] - 8 * jj
    return jj + (t + (r + 64 - t) % 8) // 8


def exchange_kernel(
    imap, mask, contrib, front,
    R, X, LR, UR, CR,
    cv, SP, M0, M1, M2, M3, S, PC, PR, FC, FR, RBr, RBx, RCr, RCx,
    ld, ldf, cs, cr, zs, zr, xs, xr, own,
    ldb, ldc, lcopy, Ls, Lr, Lxs, Lcs, Lcr, L3s,
    Us, Ur, Ups, ucopy, Cs, Cr, Cps, ccopy, Ccs, Ccr,
):
    M = [M0, M1, M2, M3]
    r = lax.axis_index("row")
    c = lax.axis_index("col")
    y, e = r // 2, r % 2
    h, z, core = c // 8, (c // 2) % 4, c % 2

    def dev(y_, e_, h_, z_, core_):
        return (2 * y_ + e_, 8 * h_ + 2 * z_ + core_)

    core_peer = dev(y, e, h, z, 1 - core)
    x_peer = dev(y, e, 1 - h, z, core)
    e_peer = dev(y, 1 - e, h, z, core)

    def z_peer(z_):
        return dev(y, e, h, z_, core)

    def y_peer(y_):
        return dev(y_, e, h, z, core)

    def remote(src, dst, ss, rs, to):
        return pltpu.make_async_remote_copy(
            src_ref=src, dst_ref=dst, send_sem=ss, recv_sem=rs, device_id=to, device_id_type=MESH
        )

    def load_c(jj):
        return pltpu.make_async_copy(contrib.at[pl.ds(jj * BS, BS)], cv.at[jj], ld.at[jj])

    for jj in range(4):
        load_c(jj).start()
    is_col_source = (h == 0) & (z < 2)
    is_row_source = r < 4
    load_fc = pltpu.make_async_copy(front.at[:, pl.ds(0, BS)], FC, ldf.at[0])
    load_fr = pltpu.make_async_copy(front.at[pl.ds(0, BS)], FR, ldf.at[1])

    @pl.when(is_col_source)
    def _():
        load_fc.start()

    @pl.when(is_row_source)
    def _():
        load_fr.start()

    barrier = pltpu.get_barrier_semaphore()
    peers = [core_peer, x_peer, e_peer]
    peers += [z_peer((z + d) % 4) for d in (1, 2, 3)]
    peers += [y_peer((y + d) % 4) for d in (1, 3)]
    for p in peers:
        pl.semaphore_signal(barrier, inc=1, device_id=p, device_id_type=MESH)
    pl.semaphore_wait(barrier, len(peers))

    t_own = imap[h, 8 * z] - 8 * z
    odd_mine = (core + t_own) % 2
    start_own = (4 * z + (t_own + odd_mine) // 2) % 8

    def core_copy(jj):
        return remote(SP.at[jj], M[jj].at[pl.ds(2 * core, 2)], cs.at[jj], cr.at[jj], core_peer)

    for jj in range(4):
        load_c(jj).wait()
        for i in range(2):
            even = cv[jj, :, 2 * i * BS:(2 * i + 1) * BS]
            odd = cv[jj, :, (2 * i + 1) * BS:(2 * i + 2) * BS]
            SP[jj, i] = jnp.where(odd_mine == 1, even, odd)
            M[jj][2 * core + i] = jnp.where(odd_mine == 1, odd, even)
        core_copy(jj).start()

    def z_copy(jj, d):
        to = (z + d) % 4
        return remote(S.at[jj, to], R.at[z, jj], zs.at[jj, d], zr.at[jj, z], z_peer(to))

    def z_wait(jj, g):
        remote(S.at[jj, 0], R.at[g, jj], zs.at[jj, 0], zr.at[jj, g], z_peer(g)).wait_recv()

    def own_copy(jj):
        return pltpu.make_async_copy(S.at[jj, z], R.at[z, jj], own.at[jj])

    def x_own(jj):
        return remote(S.at[jj, z], X.at[z, jj], xs.at[jj, z], xr.at[jj, z], x_peer)

    def x_copy(jj, g):
        return remote(R.at[g, jj], X.at[g, jj], xs.at[jj, g], xr.at[jj, g], x_peer)

    def forward_x(jj, d):
        g = (z + d) % 4
        z_wait(jj, g)
        x_copy(jj, g).start()

    for jj in range(4):
        core_copy(jj).wait_recv()
        for to in range(4):
            S[jj, to] = M[jj][(to + 8 - start_own) % 4]
        own_copy(jj).start()
        for d in (1, 3, 2):
            z_copy(jj, d).start()
        if jj == 0:
            x_own(jj).start()

    for d in (1, 3, 2):
        forward_x(0, d)
    for jj in range(1, 4):
        x_own(jj).start()
    for jj in range(4):
        own_copy(jj).wait()

    def u_next(k, half):
        s = k // 2
        d = 1 if half == 0 else -1
        return y_peer((y + 4 + d) % 4)

    def u_copy(k, half, src):
        return remote(
            src, UR.at[k, pl.ds(half * 128, 128)], Us.at[k, half], Ur.at[k, half], u_next(k, half)
        )

    def u_partner(half):
        return remote(
            PR.at[pl.ds(half * 128, 128)], UR.at[r, pl.ds(half * 128, 128)],
            Ups.at[half], Ur.at[r, half], e_peer,
        )

    own_u = pltpu.make_async_copy(PR, UR.at[jnp.minimum(r, 3)], ucopy.at[0])

    @pl.when(is_row_source)
    def _():
        for g in range(4):
            x_copy(0, g).wait_recv()
        for g in range(4):
            pltpu.make_async_copy(R.at[g, 0], RBr.at[g], ldb.at[0, g]).start()
            pltpu.make_async_copy(X.at[g, 0], RBx.at[g], ldb.at[1, g]).start()
        load_fr.wait()
        for g in range(4):
            pltpu.make_async_copy(R.at[g, 0], RBr.at[g], ldb.at[0, g]).wait()
            pltpu.make_async_copy(X.at[g, 0], RBx.at[g], ldb.at[1, g]).wait()
        row_in = [(local_row(imap, child, 0, r) == 0) for child in (h, 1 - h)]
        hit = []
        for g in range(4):
            for w, child in enumerate((h, 1 - h)):
                lands, lc = place(imap, child, g, h, z, core)
                hit.append((w, g, lands & row_in[w], lc))
        for lc in range(4):
            weights = [(w, g, jnp.where(ok & (at == lc), 1.0, 0.0).astype(f32)) for w, g, ok, at in hit]
            present = mask[r, c + 16 * lc].astype(f32)

            @pl.loop(0, 8)
            def _(q):
                rows = pl.ds(pl.multiple_of(q * 32, 32), 32)
                total = FR[rows, lc * BS:(lc + 1) * BS]
                for w, g, weight in weights:
                    total = total + weight * (RBr if w == 0 else RBx)[g, rows, :]
                PR[rows, lc * BS:(lc + 1) * BS] = total * present
        own_u.start()
        for half in range(2):
            u_partner(half).start()
            u_copy(r, half, PR.at[pl.ds(half * 128, 128)]).start()

    @pl.when(z != 0)
    def _():
        for jj in range(1, 4):
            z_wait(jj, 0)
            x_copy(jj, 0).start()

    panel = 2 * z + core

    def l_next(l):
        return z_peer((z + (1 if l % 2 == 0 else 3)) % 4)

    def l_copy(s, l, src):
        return remote(src, LR.at[2 * s + core, l], Ls.at[s, l], Lr.at[s, l], l_next(l))

    def l_wait(s, l):
        l_copy(s, l, LR.at[2 * s + core, l]).wait_recv()

    def l_x(s, l):
        return remote(
            LR.at[2 * s + core, l], LR.at[2 * s + core, l], Lxs.at[s, l], Lr.at[s, l], x_peer
        )

    def l_x_source(l):
        return remote(PC.at[l], LR.at[panel, l], Lxs.at[z, l], Lr.at[z, l], x_peer)

    def l_core(s, l):
        return remote(
            LR.at[2 * s + core, l], LR.at[2 * s + core, l], Lcs.at[s, l], Lcr.at[s, l], core_peer
        )

    def l_three(s, l, d):
        return remote(
            LR.at[2 * s + core, l], LR.at[2 * s + core, l],
            L3s.at[s, l, d], Lr.at[s, l], z_peer((z + d) % 4),
        )

    shift = [0, 0, 1, 3, 1, 3, 2, 2]
    own_l = pltpu.make_async_copy(PC, LR.at[jnp.minimum(panel, 3)], lcopy.at[0])

    @pl.when(is_col_source)
    def _():
        @pl.when(z == 0)
        def _():
            for jj in range(4):
                if jj > 0:
                    x_copy(jj, 0).wait_recv()

        @pl.when(z != 0)
        def _():
            for jj in range(1, 4):
                x_copy(jj, 0).wait_recv()

        @pl.when(r >= 4)
        def _():
            x_copy(0, 0).wait_recv()

        from_r = pltpu.make_async_copy(R.at[0], RCr, ldc.at[0])
        from_x = pltpu.make_async_copy(X.at[0], RCx, ldc.at[1])
        from_r.start()
        from_x.start()
        load_fc.wait()
        from_r.wait()
        from_x.wait()
        hits = [place(imap, child, 0, h, z, core) for child in (h, 1 - h)]
        rows_at = [[local_row(imap, child, jj, r) for jj in range(4)] for child in (h, 1 - h)]
        for l in range(8):
            present = mask[r + 8 * l, c].astype(f32)
            total = FC[l * BS:(l + 1) * BS, :]
            for w, source in enumerate((RCr, RCx)):
                lands, lc = hits[w]
                index = jnp.int32(0)
                found = jnp.int32(0)
                for jj in range(4):
                    here = (rows_at[w][jj] == l).astype(jnp.int32)
                    index = jnp.where(here > 0, jj, index)
                    found = found + here
                weight = jnp.where(lands & (lc == 0) & (found > 0), 1.0, 0.0).astype(f32)
                total = total + weight * source[index]
            PC[l] = total * present
            l_copy(z, l, PC.at[l]).start()
            if shift[l] == 0:
                l_x_source(l).start()
        own_l.start()

    for jj in range(1, 4):
        for d in (1, 3, 2):
            g = (z + d) % 4

            @pl.when(g != 0)
            def _():
                z_wait(jj, g)
                x_copy(jj, g).start()

    @pl.when(is_col_source)
    def _():
        own_l.wait()

    def at_source(s):
        return (h == 0) & (z == s)

    def column_step(s, l):
        dist = (z + 4 - s) % 4 if l % 2 == 0 else (s + 4 - z) % 4
        cross_z = (s + shift[l]) % 4

        @pl.when(jnp.logical_not(at_source(s)))
        def _():
            l_wait(s, l)

        @pl.when(h == 0)
        def _():
            @pl.when((dist > 0) & (dist < 3))
            def _():
                l_copy(s, l, LR.at[2 * s + core, l]).start()

            if shift[l] != 0:
                @pl.when(z == cross_z)
                def _():
                    l_x(s, l).start()

        @pl.when((h == 1) & (z == cross_z))
        def _():
            for d in (1, 3, 2):
                l_three(s, l, d).start()

        l_core(s, l).start()

    def c_next(s):
        return y_peer((y + (1 if s == 0 else 3)) % 4)

    def c_copy(k, s, src):
        return remote(src, CR.at[k, core, s], Cs.at[k, s], Cr.at[k, s], c_next(s))

    def c_partner(s):
        return remote(LR.at[2 * s + core, 0], CR.at[r, core, s], Cps.at[s], Cr.at[r, s], e_peer)

    def c_own(s):
        return pltpu.make_async_copy(
            LR.at[2 * s + core, 0], CR.at[jnp.minimum(r, 3), core, s], ccopy.at[s]
        )

    def c_core(k):
        return remote(CR.at[k, core], CR.at[k, core], Ccs.at[k], Ccr.at[k], core_peer)

    def ring_dist(k, way):
        s = k // 2
        return (y + 4 - s) % 4 if way == 0 else (s + 4 - y) % 4

    def row_step(k, half):
        dist = ring_dist(k, half)

        @pl.when(r != k)
        def _():
            u_copy(k, half, UR.at[k, pl.ds(half * 128, 128)]).wait_recv()

            @pl.when(dist < 3)
            def _():
                u_copy(k, half, UR.at[k, pl.ds(half * 128, 128)]).start()

    def corner_step(k, s):
        dist = ring_dist(k, s)

        @pl.when(r != k)
        def _():
            c_copy(k, s, CR.at[k, core, s]).wait_recv()

            @pl.when(dist < 3)
            def _():
                c_copy(k, s, CR.at[k, core, s]).start()

    for s in range(2):
        column_step(s, 0)

    @pl.when(is_row_source)
    def _():
        for s in range(2):
            c_own(s).start()
            c_partner(s).start()
            c_copy(r, s, LR.at[2 * s + core, 0]).start()

    for s in range(2):
        column_step(s, 1)
    for k in range(4):
        for half in range(2):
            row_step(k, half)
    for l in (2, 3):
        for s in range(2):
            column_step(s, l)
    for k in range(4):
        for s in range(2):
            corner_step(k, s)

        @pl.when(r == k)
        def _():
            for s in range(2):
                c_own(s).wait()

        c_core(k).start()
    for l in (4, 5, 6, 7):
        for s in range(2):
            column_step(s, l)

    for jj in range(4):
        core_copy(jj).wait_send()
        for d in (1, 2, 3):
            z_copy(jj, d).wait_send()
        for g in range(4):
            x_copy(jj, g).wait_send()

    for g in range(4):
        for jj in range(4):
            done = jnp.bool_(False)
            if jj == 0:
                done = is_row_source | ((g == 0) & is_col_source)
            elif g == 0:
                done = is_col_source

            @pl.when(jnp.logical_not(done))
            def _():
                x_copy(jj, g).wait_recv()

    @pl.when(is_row_source)
    def _():
        own_u.wait()
        for half in range(2):
            u_partner(half).wait_send()
            u_copy(r, half, PR.at[pl.ds(half * 128, 128)]).wait_send()
        for s in range(2):
            c_partner(s).wait_send()
            c_copy(r, s, LR.at[2 * s + core, 0]).wait_send()
    for k in range(4):
        for way in range(2):
            dist = ring_dist(k, way)

            @pl.when((r != k) & (dist < 3))
            def _():
                u_copy(k, way, UR.at[k, pl.ds(way * 128, 128)]).wait_send()
                c_copy(k, way, CR.at[k, core, way]).wait_send()

        c_core(k).wait()
    for s in range(2):
        for l in range(8):
            dist = (z + 4 - s) % 4 if l % 2 == 0 else (s + 4 - z) % 4
            cross_z = (s + shift[l]) % 4

            @pl.when(h == 0)
            def _():
                @pl.when(dist < 3)
                def _():
                    l_copy(s, l, LR.at[2 * s + core, l]).wait_send()

                @pl.when(z == cross_z)
                def _():
                    l_x(s, l).wait_send()

            @pl.when((h == 1) & (z == cross_z))
            def _():
                for d in (1, 3, 2):
                    l_three(s, l, d).wait_send()

            l_core(s, l).wait()


def split(a):
    hi = a.astype(bf16)
    return hi, (a - hi.astype(f32)).astype(bf16)


def dot3(a, b):
    ah, al = a
    bh, bl = b
    d = functools.partial(jnp.dot, preferred_element_type=f32)
    return d(ah, bh) + (d(ah, bl) + d(al, bh))


def panel_kernel(pos, CR, UR, pinv, Vh, Vl, frow, PB, U):
    r, c = pos[0], pos[1]
    for k in range(4):
        for j in range(4):
            PB[k * BS:(k + 1) * BS, j * BS:(j + 1) * BS] = CR[k, j % 2, j // 2]
        U[k * BS:(k + 1) * BS, :] = UR[k]
    for k in range(3):
        at, rest = k * BS, (k + 1) * BS
        lower = dot3(split(PB[rest:, at:rest]), split(pinv[k]))
        PB[rest:, at:rest] = lower
        low = split(lower)
        PB[rest:, rest:] = PB[rest:, rest:] - dot3(low, split(PB[at:rest, rest:]))
        U[rest:, :] = U[rest:, :] - dot3(low, split(U[at:rest, :]))

    @pl.when(r < 4)
    def _():
        rows = pl.ds(pl.multiple_of(r * BS, BS), BS)
        frow[...] = U[rows, :]

        @pl.when(c < 4)
        def _():
            frow[:, 0:BS] = PB[rows, pl.ds(pl.multiple_of(c * BS, BS), BS)]

    @pl.when(r >= 4)
    def _():
        frow[...] = jnp.zeros_like(frow)

    @pl.when(c < 4)
    def _():
        on = lax.broadcasted_iota(jnp.int32, (K * BS, BS), 0)
        across = lax.broadcasted_iota(jnp.int32, (K * BS, BS), 1)
        U[:, 0:BS] = jnp.where(on == across + c * BS, -1.0, 0.0).astype(f32)

    for m in range(3, -1, -1):
        at, rest = m * BS, (m + 1) * BS
        total = U[at:rest, :]
        if m < 3:
            total = total - dot3(split(PB[at:rest, rest:]), (Vh[rest:, :], Vl[rest:, :]))
        vh, vl = split(dot3(split(pinv[m]), split(total)))
        Vh[at:rest, :] = vh
        Vl[at:rest, :] = vl


def child_row(imap, pos, child, l):
    index = jnp.int32(0)
    found = jnp.int32(0)
    for jj in range(4):
        here = (local_row(imap, child, jj, pos[0]) == l).astype(jnp.int32)
        index = jnp.where(here > 0, jj, index)
        found = found + here
    return index, found


def update_kernel(imap, mask, pos, F, LRl, R, X, Vh, Vl, frow, out, acc, ah, al):
    l = pl.program_id(0)
    r, c = pos[0], pos[1]
    h, z, core = c // 8, (c // 2) % 4, c % 2
    for lc in range(4):
        acc[lc] = F[:, lc * BS:(lc + 1) * BS]
    for child, source in ((h, R), (1 - h, X)):
        _, found = child_row(imap, pos, child, l)
        for g in range(4):
            lands, lc = place(imap, child, g, h, z, core)

            @pl.when(lands & (found > 0))
            def _():
                acc[lc] = acc[lc] + source[g, 0]
    for p in range(4):
        hi, lo = split(LRl[p, 0])
        ah[:, p * BS:(p + 1) * BS] = hi
        al[:, p * BS:(p + 1) * BS] = lo
    for lc in range(4):
        present = mask[r + 8 * l, c + 16 * lc].astype(f32)
        if lc == 0:
            present = present * (c >= 4).astype(f32)
        cols = slice(lc * BS, (lc + 1) * BS)
        product = dot3((ah[...], al[...]), (Vh[:, cols], Vl[:, cols]))
        out[:, cols] = acc[lc] * present - product

    @pl.when((l == 0) & (r < 4))
    def _():
        out[...] = frow[...]


def body(front, contrib, pivot_inverse, index_map, fill_mask):
    r = lax.axis_index("row")
    c = lax.axis_index("col")
    pos = jnp.stack([r, c]).astype(jnp.int32)
    any_ = pl.BlockSpec(memory_space=pl.ANY)
    smem = pl.BlockSpec(memory_space=pltpu.SMEM)
    vmem = pl.BlockSpec(memory_space=pltpu.VMEM)
    V = pltpu.VMEM
    dma = pltpu.SemaphoreType.DMA
    blk = (BS, BS)
    R, X, LR, UR, CR = pl.pallas_call(
        exchange_kernel,
        out_shape=[
            jax.ShapeDtypeStruct((4, 4) + blk, f32),
            jax.ShapeDtypeStruct((4, 4) + blk, f32),
            jax.ShapeDtypeStruct((4, 8) + blk, f32),
            jax.ShapeDtypeStruct((4, BS, 4 * BS), f32),
            jax.ShapeDtypeStruct((4, 2, 2) + blk, f32),
        ],
        in_specs=[smem, smem, any_, any_],
        out_specs=[any_] * 5,
        scratch_shapes=[
            V((4, BS, 4 * BS), f32), V((4, 2) + blk, f32),
            V((4,) + blk, f32), V((4,) + blk, f32), V((4,) + blk, f32), V((4,) + blk, f32),
            V((4, 4) + blk, f32), V((8,) + blk, f32), V((BS, 4 * BS), f32),
            V((8 * BS, BS), f32), V((BS, 4 * BS), f32),
            V((4,) + blk, f32), V((4,) + blk, f32), V((4,) + blk, f32), V((4,) + blk, f32),
            dma((4,)), dma((2,)), dma((4,)), dma((4,)), dma((4, 4)), dma((4, 4)), dma((4, 4)),
            dma((4, 4)), dma((4,)),
            dma((2, 4)), dma((2,)), dma((1,)), dma((2, 8)), dma((2, 8)), dma((2, 8)), dma((2, 8)),
            dma((2, 8)), dma((2, 8, 4)),
            dma((4, 2)), dma((4, 2)), dma((2,)), dma((1,)), dma((4, 2)), dma((4, 2)), dma((2,)),
            dma((2,)), dma((4,)), dma((4,)),
        ],
        compiler_params=pltpu.CompilerParams(
            collective_id=0, has_side_effects=True, vmem_limit_bytes=48 * 2**20
        ),
        name="exchange",
    )(index_map, fill_mask, contrib, front)

    Vh, Vl, frow = pl.pallas_call(
        panel_kernel,
        out_shape=[
            jax.ShapeDtypeStruct((4 * BS, 4 * BS), bf16),
            jax.ShapeDtypeStruct((4 * BS, 4 * BS), bf16),
            jax.ShapeDtypeStruct((BS, 4 * BS), f32),
        ],
        in_specs=[smem, vmem, vmem, vmem],
        out_specs=[vmem] * 3,
        scratch_shapes=[V((4 * BS, 4 * BS), f32), V((4 * BS, 4 * BS), f32)],
        compiler_params=pltpu.CompilerParams(vmem_limit_bytes=56 * 2**20),
        name="panel",
    )(pos, CR, UR, pivot_inverse)

    def child_spec(own):
        def index(l, imap, mask, pos):
            child = pos[1] // 8
            if not own:
                child = 1 - child
            return 0, child_row(imap, pos, child, l)[0], 0, 0

        return pl.BlockSpec((4, 1) + blk, index)

    return pl.pallas_call(
        update_kernel,
        out_shape=jax.ShapeDtypeStruct(front.shape, f32),
        grid_spec=pltpu.PrefetchScalarGridSpec(
            num_scalar_prefetch=3,
            grid=(8,),
            in_specs=[
                pl.BlockSpec((BS, 4 * BS), lambda l, *_: (l, 0)),
                pl.BlockSpec((4, 1) + blk, lambda l, *_: (0, l, 0, 0)),
                child_spec(True),
                child_spec(False),
                pl.BlockSpec((4 * BS, 4 * BS), lambda l, *_: (0, 0)),
                pl.BlockSpec((4 * BS, 4 * BS), lambda l, *_: (0, 0)),
                pl.BlockSpec((BS, 4 * BS), lambda l, *_: (0, 0)),
            ],
            out_specs=pl.BlockSpec((BS, 4 * BS), lambda l, *_: (l, 0)),
            scratch_shapes=[V((4,) + blk, f32), V((BS, 4 * BS), bf16), V((BS, 4 * BS), bf16)],
        ),
        compiler_params=pltpu.CompilerParams(vmem_limit_bytes=48 * 2**20),
        name="update",
    )(index_map, fill_mask, pos, front, LR, R, X, Vh, Vl, frow)


def solution(mesh):
    in_specs = (P("row", "col"), P("row", "col"), P(), P(), P())
    out_specs = P("row", "col")
    return jax.shard_map(body, mesh=mesh, in_specs=in_specs, out_specs=out_specs, check_vma=False)
```

```python
import functools

import jax
import jax.numpy as jnp
from jax import lax
from jax.experimental import pallas as pl
from jax.experimental.pallas import tpu as pltpu
from jax.sharding import PartitionSpec as P

BS = 256
K = 4
FREE = False
PARTS = "XULC"
MESH = pl.DeviceIdType.MESH
f32 = jnp.float32
bf16 = jnp.bfloat16


def place(imap, child, g, h, z, core):
    t = imap[child, 8 * g] - 8 * g
    first = (core + t) % 2
    start = (4 * g + (t + first) // 2) % 8
    m = (z + 8 - start) % 4
    half = ((start + m) % 8) // 4
    block = 8 * g + t + first + 2 * m
    return half == h, block // 16


def local_row(imap, child, jj, r):
    t = imap[child, 8 * jj] - 8 * jj
    return jj + (t + (r + 64 - t) % 8) // 8


def exchange_kernel(
    free, parts, imap, mask, contrib, front,
    R, X, LR, UR, CR,
    cv, SP, M0, M1, M2, M3, S, PC, PR, FC, FR, RBr, RBx, RCr, RCx,
    ld, ldf, cs, cr, zs, zr, xs, xr, own,
    ldb, ldc, lcopy, Ls, Lr, Lxs, Lcs, Lcr, L3s,
    Us, Ur, Ups, ucopy, Cs, Cr, Cps, ccopy, Ccs, Ccr,
):
    M = [M0, M1, M2, M3]
    r = lax.axis_index("row")
    c = lax.axis_index("col")
    y, e = r // 2, r % 2
    h, z, core = c // 8, (c // 2) % 4, c % 2

    def dev(y_, e_, h_, z_, core_):
        return (2 * y_ + e_, 8 * h_ + 2 * z_ + core_)

    core_peer = dev(y, e, h, z, 1 - core)
    x_peer = dev(y, e, 1 - h, z, core)
    e_peer = dev(y, 1 - e, h, z, core)

    def z_peer(z_):
        return dev(y, e, h, z_, core)

    def y_peer(y_):
        return dev(y_, e, h, z, core)

    def remote(src, dst, ss, rs, to):
        return pltpu.make_async_remote_copy(
            src_ref=src, dst_ref=dst, send_sem=ss, recv_sem=rs, device_id=to, device_id_type=MESH
        )

    def load_c(jj):
        return pltpu.make_async_copy(contrib.at[pl.ds(jj * BS, BS)], cv.at[jj], ld.at[jj])

    for jj in range(4) if "X" in parts else ():
        load_c(jj).start()
    has = {name: name in parts for name in "XULC"}
    never = jnp.bool_(False)
    is_col_source = (h == 0) & (z < 2) if has["L"] else never
    is_row_source = r < 4 if has["U"] else never
    load_fc = pltpu.make_async_copy(front.at[:, pl.ds(0, BS)], FC, ldf.at[0])
    load_fr = pltpu.make_async_copy(front.at[pl.ds(0, BS)], FR, ldf.at[1])

    @pl.when(is_col_source)
    def _():
        load_fc.start()

    @pl.when(is_row_source)
    def _():
        load_fr.start()

    barrier = pltpu.get_barrier_semaphore()
    peers = [core_peer, x_peer, e_peer]
    peers += [z_peer((z + d) % 4) for d in (1, 2, 3)]
    peers += [y_peer((y + d) % 4) for d in (1, 3)]
    for p in peers:
        pl.semaphore_signal(barrier, inc=1, device_id=p, device_id_type=MESH)
    pl.semaphore_wait(barrier, len(peers))

    t_own = imap[h, 8 * z] - 8 * z
    odd_mine = (core + t_own) % 2
    start_own = (4 * z + (t_own + odd_mine) // 2) % 8

    def core_copy(jj):
        return remote(SP.at[jj], M[jj].at[pl.ds(2 * core, 2)], cs.at[jj], cr.at[jj], core_peer)

    def z_copy(jj, d):
        to = (z + d) % 4
        return remote(S.at[jj, to], R.at[z, jj], zs.at[jj, d], zr.at[jj, z], z_peer(to))

    def z_wait(jj, g):
        remote(S.at[jj, 0], R.at[g, jj], zs.at[jj, 0], zr.at[jj, g], z_peer(g)).wait_recv()

    def own_copy(jj):
        return pltpu.make_async_copy(S.at[jj, z], R.at[z, jj], own.at[jj])

    def x_own(jj):
        return remote(S.at[jj, z], X.at[z, jj], xs.at[jj, z], xr.at[jj, z], x_peer)

    def x_copy(jj, g):
        return remote(R.at[g, jj], X.at[g, jj], xs.at[jj, g], xr.at[jj, g], x_peer)

    def forward_x(jj, d):
        g = (z + d) % 4
        z_wait(jj, g)
        x_copy(jj, g).start()

    def swap_cores():
        for jj in range(4):
            load_c(jj).wait()
            for i in range(2):
                even = cv[jj, :, 2 * i * BS:(2 * i + 1) * BS]
                odd = cv[jj, :, (2 * i + 1) * BS:(2 * i + 2) * BS]
                SP[jj, i] = jnp.where(odd_mine == 1, even, odd)
                M[jj][2 * core + i] = jnp.where(odd_mine == 1, odd, even)
            core_copy(jj).start()

    def arrange(jj):
        core_copy(jj).wait_recv()
        for to in range(4):
            S[jj, to] = M[jj][(to + 8 - start_own) % 4]
        own_copy(jj).start()
        for d in (1, 3, 2):
            z_copy(jj, d).start()

    def own_waits():
        for jj in range(4):
            own_copy(jj).wait()

    def y_next(way):
        return y_peer((y + (1 if way == 0 else 3)) % 4)

    def u_rows(way, q):
        return pl.ds(way * 128 + q * 64, 64)

    def u_copy(k, way, q, src):
        return remote(
            src, UR.at[k, u_rows(way, q)], Us.at[k, way, q], Ur.at[k, way, q], y_next(way)
        )

    def u_held(k, way, q):
        return UR.at[k, u_rows(way, q)]

    def u_partner(way, q):
        return remote(
            PR.at[u_rows(way, q)], UR.at[r, u_rows(way, q)],
            Ups.at[way, q], Ur.at[r, way, q], e_peer,
        )

    own_u = pltpu.make_async_copy(PR, UR.at[jnp.minimum(r, 3)], ucopy.at[0])

    def send_row_panel():
        own_u.start()
        for q in range(2):
            for way in range(2):
                u_partner(way, q).start()
                u_copy(r, way, q, PR.at[u_rows(way, q)]).start()

    def make_row_panel():
        @pl.when(is_row_source)
        def _():
            for g in range(4):
                x_copy(0, g).wait_recv()
            for g in range(4):
                pltpu.make_async_copy(R.at[g, 0], RBr.at[g], ldb.at[0, g]).start()
                pltpu.make_async_copy(X.at[g, 0], RBx.at[g], ldb.at[1, g]).start()
            load_fr.wait()
            for g in range(4):
                pltpu.make_async_copy(R.at[g, 0], RBr.at[g], ldb.at[0, g]).wait()
                pltpu.make_async_copy(X.at[g, 0], RBx.at[g], ldb.at[1, g]).wait()
            row_in = [(local_row(imap, child, 0, r) == 0) for child in (h, 1 - h)]
            hit = []
            for g in range(4):
                for w, child in enumerate((h, 1 - h)):
                    lands, lc = place(imap, child, g, h, z, core)
                    hit.append((w, g, lands & row_in[w], lc))
            for lc in range(4):
                weights = [(w, g, jnp.where(ok & (at == lc), 1.0, 0.0).astype(f32)) for w, g, ok, at in hit]
                present = mask[r, c + 16 * lc].astype(f32)

                @pl.loop(0, 8)
                def _(q):
                    rows = pl.ds(pl.multiple_of(q * 32, 32), 32)
                    total = FR[rows, lc * BS:(lc + 1) * BS]
                    for w, g, weight in weights:
                        total = total + weight * (RBr if w == 0 else RBx)[g, rows, :]
                    PR[rows, lc * BS:(lc + 1) * BS] = total * present
            send_row_panel()

    def make_row_panel_free():
        @pl.when(is_row_source)
        def _():
            load_fr.wait()
            for lc in range(4):
                PR[:, lc * BS:(lc + 1) * BS] = (
                    FR[:, lc * BS:(lc + 1) * BS] * mask[r, c + 16 * lc].astype(f32)
                )
            send_row_panel()

    panel = 2 * z + core

    def l_next(l):
        return z_peer((z + (1 if l % 2 == 0 else 3)) % 4)

    def l_copy(s, l, src):
        return remote(src, LR.at[2 * s + core, l], Ls.at[s, l], Lr.at[s, l], l_next(l))

    def l_wait(s, l):
        l_copy(s, l, LR.at[2 * s + core, l]).wait_recv()

    def l_x(s, l):
        return remote(
            LR.at[2 * s + core, l], LR.at[2 * s + core, l], Lxs.at[s, l], Lr.at[s, l], x_peer
        )

    def l_x_source(l):
        return remote(PC.at[l], LR.at[panel, l], Lxs.at[z, l], Lr.at[z, l], x_peer)

    def l_core(s, l):
        return remote(
            LR.at[2 * s + core, l], LR.at[2 * s + core, l], Lcs.at[s, l], Lcr.at[s, l], core_peer
        )

    def l_three(s, l, d):
        return remote(
            LR.at[2 * s + core, l], LR.at[2 * s + core, l],
            L3s.at[s, l, d], Lr.at[s, l], z_peer((z + d) % 4),
        )

    shift = [0, 0, 1, 3, 1, 3, 2, 2]
    own_l = pltpu.make_async_copy(PC, LR.at[jnp.minimum(panel, 3)], lcopy.at[0])

    def send_column_block(l, value):
        PC[l] = value
        l_copy(z, l, PC.at[l]).start()
        if shift[l] == 0:
            l_x_source(l).start()

    def make_column_panel():
        @pl.when(is_col_source)
        def _():
            @pl.when(z == 0)
            def _():
                for jj in range(4):
                    if jj > 0:
                        x_copy(jj, 0).wait_recv()

            @pl.when(z != 0)
            def _():
                for jj in range(1, 4):
                    x_copy(jj, 0).wait_recv()

            @pl.when(r >= 4)
            def _():
                x_copy(0, 0).wait_recv()

            from_r = pltpu.make_async_copy(R.at[0], RCr, ldc.at[0])
            from_x = pltpu.make_async_copy(X.at[0], RCx, ldc.at[1])
            from_r.start()
            from_x.start()
            load_fc.wait()
            from_r.wait()
            from_x.wait()
            hits = [place(imap, child, 0, h, z, core) for child in (h, 1 - h)]
            rows_at = [[local_row(imap, child, jj, r) for jj in range(4)] for child in (h, 1 - h)]
            for l in range(8):
                present = mask[r + 8 * l, c].astype(f32)
                total = FC[l * BS:(l + 1) * BS, :]
                for w, source in enumerate((RCr, RCx)):
                    lands, lc = hits[w]
                    index = jnp.int32(0)
                    found = jnp.int32(0)
                    for jj in range(4):
                        here = (rows_at[w][jj] == l).astype(jnp.int32)
                        index = jnp.where(here > 0, jj, index)
                        found = found + here
                    weight = jnp.where(lands & (lc == 0) & (found > 0), 1.0, 0.0).astype(f32)
                    total = total + weight * source[index]
                send_column_block(l, total * present)
            own_l.start()

    def make_column_panel_free():
        @pl.when(is_col_source)
        def _():
            load_fc.wait()
            for l in range(8):
                send_column_block(l, FC[l * BS:(l + 1) * BS, :] * mask[r + 8 * l, c].astype(f32))
            own_l.start()

    def group0_early():
        @pl.when(z != 0)
        def _():
            for jj in range(1, 4):
                z_wait(jj, 0)
                x_copy(jj, 0).start()

    def rest_x(jj):
        for d in (1, 3, 2):
            g = (z + d) % 4

            @pl.when(g != 0)
            def _():
                z_wait(jj, g)
                x_copy(jj, g).start()

    def own_l_wait():
        @pl.when(is_col_source)
        def _():
            own_l.wait()

    def column_ring(step):
        for i in range(4):
            if not 1 <= step - i <= 3:
                continue
            for way in range(2):
                l = 2 * i + way
                for s in range(2):
                    dist = (z + 4 - s) % 4 if way == 0 else (s + 4 - z) % 4

                    @pl.when(dist == step - i)
                    def _():
                        l_wait(s, l)
                        if step - i < 3:
                            l_copy(s, l, LR.at[2 * s + core, l]).start()
                        if shift[l] != 0:
                            @pl.when(z == (s + shift[l]) % 4)
                            def _():
                                l_x(s, l).start()

                        l_core(s, l).start()

    def column_spread(l):
        for s in range(2):
            @pl.when(z == (s + shift[l]) % 4)
            def _():
                l_wait(s, l)
                for d in (1, 3, 2):
                    l_three(s, l, d).start()
                l_core(s, l).start()

    def column_rest(l):
        for s in range(2):
            @pl.when(z != (s + shift[l]) % 4)
            def _():
                l_wait(s, l)
                l_core(s, l).start()

    def column_slot(slot):
        @pl.when(h == 0)
        def _():
            if slot == 1:
                own_l_wait()
                for l in range(8):
                    @pl.when(z < 2)
                    def _():
                        l_core(z, l).start()

            column_ring(slot)
            if slot == 3 and has["C"]:
                corner_start()

        @pl.when(h == 1)
        def _():
            if slot == 1:
                column_spread(0)
                column_spread(1)
            if slot == 2:
                column_rest(0)
                if has["C"]:
                    corner_start()
            if slot == 3:
                column_spread(2)
                column_spread(3)
                column_rest(1)
            if slot == 4:
                column_spread(4)
                column_spread(5)
                column_rest(2)
                column_rest(3)
            if slot == 5:
                column_rest(4)
                column_rest(5)
            if slot == 6:
                column_spread(6)
                column_spread(7)
                column_rest(6)
                column_rest(7)

    def c_held(k, s, q):
        return CR.at[k, core, s, pl.ds(128 * q, 128)]

    def c_from(s, q):
        return LR.at[2 * s + core, 0, pl.ds(128 * q, 128)]

    def c_copy(k, s, q, src):
        return remote(src, c_held(k, s, q), Cs.at[k, s, q], Cr.at[k, s, q], y_next(s))

    def c_partner(s, q):
        return remote(c_from(s, q), c_held(r, s, q), Cps.at[s, q], Cr.at[r, s, q], e_peer)

    def c_own(s):
        return pltpu.make_async_copy(
            LR.at[2 * s + core, 0], CR.at[jnp.minimum(r, 3), core, s], ccopy.at[s]
        )

    def c_core(k):
        return remote(CR.at[k, core], CR.at[k, core], Ccs.at[k], Ccr.at[k], core_peer)

    def ring_dist(k, way):
        s = k // 2
        return (y + 4 - s) % 4 if way == 0 else (s + 4 - y) % 4

    def row_ring(step):
        for q in range(2):
            if not 0 <= step - q <= 3:
                continue
            for k in range(4):
                for way in range(2):
                    @pl.when((r != k) & (ring_dist(k, way) == step - q))
                    def _():
                        u_copy(k, way, q, u_held(k, way, q)).wait_recv()
                        if step - q < 3:
                            u_copy(k, way, q, u_held(k, way, q)).start()

    def corner_ring(step):
        for q in range(2):
            if not 0 <= step - q <= 3:
                continue
            for k in range(4):
                for s in range(2):
                    @pl.when((r != k) & (ring_dist(k, s) == step - q))
                    def _():
                        c_copy(k, s, q, c_held(k, s, q)).wait_recv()
                        if step - q < 3:
                            c_copy(k, s, q, c_held(k, s, q)).start()

    def corner_start():
        @pl.when(is_row_source)
        def _():
            for q in range(2):
                for s in range(2):
                    c_partner(s, q).start()
                    c_copy(r, s, q, c_from(s, q)).start()
            for s in range(2):
                c_own(s).start()

    def corner_swap():
        @pl.when(is_row_source)
        def _():
            for s in range(2):
                c_own(s).wait()

        for k in range(4):
            c_core(k).start()

    def slots(free):
        for slot in range(1, 7):
            if has["L"]:
                column_slot(slot)
            if has["U"] and slot <= 5:
                row_ring(slot - 1)
            if has["X"]:
                if free:
                    if slot == 2:
                        own_waits()
                    if 2 <= slot <= 5:
                        for d in (1, 3, 2):
                            forward_x(slot - 2, d)
                elif slot <= 3:
                    rest_x(slot)
            if has["C"]:
                for step in {4: (0,), 5: (1,), 6: (2, 3, 4)}.get(slot, ()):
                    corner_ring(step)
        if has["C"]:
            corner_swap()

    if free:
        if has["L"]:
            make_column_panel_free()
        if has["U"]:
            make_row_panel_free()
        if has["X"]:
            swap_cores()
            for jj in range(4):
                arrange(jj)
                x_own(jj).start()
    else:
        swap_cores()
        for jj in range(4):
            arrange(jj)
            if jj == 0:
                x_own(jj).start()
        for d in (1, 3, 2):
            forward_x(0, d)
        group0_early()
        for jj in range(1, 4):
            x_own(jj).start()
        own_waits()
        if has["U"]:
            make_row_panel()
        if has["L"]:
            make_column_panel()
    slots(free)

    for jj in range(4) if has["X"] else ():
        core_copy(jj).wait_send()
        for d in (1, 2, 3):
            z_copy(jj, d).wait_send()
        for g in range(4):
            x_copy(jj, g).wait_send()

    for g in range(4) if has["X"] else ():
        for jj in range(4):
            done = never
            if free:
                pass
            elif jj == 0:
                done = is_row_source | ((g == 0) & is_col_source)
            elif g == 0:
                done = is_col_source

            @pl.when(jnp.logical_not(done))
            def _():
                x_copy(jj, g).wait_recv()

    @pl.when(is_row_source)
    def _():
        own_u.wait()
        for q in range(2):
            for way in range(2):
                u_partner(way, q).wait_send()
                u_copy(r, way, q, PR.at[u_rows(way, q)]).wait_send()
                if has["C"]:
                    c_partner(way, q).wait_send()
                    c_copy(r, way, q, c_from(way, q)).wait_send()
    for k in range(4) if has["U"] else ():
        for way in range(2):
            dist = ring_dist(k, way)

            @pl.when((r != k) & (dist < 3))
            def _():
                for q in range(2):
                    u_copy(k, way, q, u_held(k, way, q)).wait_send()
                    if has["C"]:
                        c_copy(k, way, q, c_held(k, way, q)).wait_send()

        if has["C"]:
            c_core(k).wait()
    for s in range(2) if has["L"] else ():
        for l in range(8):
            dist = (z + 4 - s) % 4 if l % 2 == 0 else (s + 4 - z) % 4
            cross_z = (s + shift[l]) % 4

            @pl.when(h == 0)
            def _():
                @pl.when(dist < 3)
                def _():
                    l_copy(s, l, LR.at[2 * s + core, l]).wait_send()

                @pl.when(z == cross_z)
                def _():
                    l_x(s, l).wait_send()

            @pl.when((h == 1) & (z == cross_z))
            def _():
                for d in (1, 3, 2):
                    l_three(s, l, d).wait_send()

            l_core(s, l).wait()


def split(a):
    hi = a.astype(bf16)
    return hi, (a - hi.astype(f32)).astype(bf16)


def dot3(a, b):
    ah, al = a
    bh, bl = b
    d = functools.partial(jnp.dot, preferred_element_type=f32)
    return d(ah, bh) + (d(ah, bl) + d(al, bh))


def panel_kernel(pos, CR, UR, pinv, Vh, Vl, frow, PB, U):
    r, c = pos[0], pos[1]
    for k in range(4):
        for j in range(4):
            PB[k * BS:(k + 1) * BS, j * BS:(j + 1) * BS] = CR[k, j % 2, j // 2]
        U[k * BS:(k + 1) * BS, :] = UR[k]
    for k in range(3):
        at, rest = k * BS, (k + 1) * BS
        lower = dot3(split(PB[rest:, at:rest]), split(pinv[k]))
        PB[rest:, at:rest] = lower
        low = split(lower)
        PB[rest:, rest:] = PB[rest:, rest:] - dot3(low, split(PB[at:rest, rest:]))
        U[rest:, :] = U[rest:, :] - dot3(low, split(U[at:rest, :]))

    @pl.when(r < 4)
    def _():
        rows = pl.ds(pl.multiple_of(r * BS, BS), BS)
        frow[...] = U[rows, :]

        @pl.when(c < 4)
        def _():
            frow[:, 0:BS] = PB[rows, pl.ds(pl.multiple_of(c * BS, BS), BS)]

    @pl.when(r >= 4)
    def _():
        frow[...] = jnp.zeros_like(frow)

    @pl.when(c < 4)
    def _():
        on = lax.broadcasted_iota(jnp.int32, (K * BS, BS), 0)
        across = lax.broadcasted_iota(jnp.int32, (K * BS, BS), 1)
        U[:, 0:BS] = jnp.where(on == across + c * BS, -1.0, 0.0).astype(f32)

    for m in range(3, -1, -1):
        at, rest = m * BS, (m + 1) * BS
        total = U[at:rest, :]
        if m < 3:
            total = total - dot3(split(PB[at:rest, rest:]), (Vh[rest:, :], Vl[rest:, :]))
        vh, vl = split(dot3(split(pinv[m]), split(total)))
        Vh[at:rest, :] = vh
        Vl[at:rest, :] = vl


def child_row(imap, pos, child, l):
    index = jnp.int32(0)
    found = jnp.int32(0)
    for jj in range(4):
        here = (local_row(imap, child, jj, pos[0]) == l).astype(jnp.int32)
        index = jnp.where(here > 0, jj, index)
        found = found + here
    return index, found


def update_kernel(imap, mask, pos, F, LRl, R, X, Vh, Vl, frow, out, acc, ah, al):
    l = pl.program_id(0)
    r, c = pos[0], pos[1]
    h, z, core = c // 8, (c // 2) % 4, c % 2
    for lc in range(4):
        acc[lc] = F[:, lc * BS:(lc + 1) * BS]
    for child, source in ((h, R), (1 - h, X)):
        _, found = child_row(imap, pos, child, l)
        for g in range(4):
            lands, lc = place(imap, child, g, h, z, core)

            @pl.when(lands & (found > 0))
            def _():
                acc[lc] = acc[lc] + source[g, 0]
    for p in range(4):
        hi, lo = split(LRl[p, 0])
        ah[:, p * BS:(p + 1) * BS] = hi
        al[:, p * BS:(p + 1) * BS] = lo
    for lc in range(4):
        present = mask[r + 8 * l, c + 16 * lc].astype(f32)
        if lc == 0:
            present = present * (c >= 4).astype(f32)
        cols = slice(lc * BS, (lc + 1) * BS)
        product = dot3((ah[...], al[...]), (Vh[:, cols], Vl[:, cols]))
        out[:, cols] = acc[lc] * present - product

    @pl.when((l == 0) & (r < 4))
    def _():
        out[...] = frow[...]


def body(front, contrib, pivot_inverse, index_map, fill_mask):
    r = lax.axis_index("row")
    c = lax.axis_index("col")
    pos = jnp.stack([r, c]).astype(jnp.int32)
    any_ = pl.BlockSpec(memory_space=pl.ANY)
    smem = pl.BlockSpec(memory_space=pltpu.SMEM)
    vmem = pl.BlockSpec(memory_space=pltpu.VMEM)
    V = pltpu.VMEM
    dma = pltpu.SemaphoreType.DMA
    blk = (BS, BS)
    R, X, LR, UR, CR = pl.pallas_call(
        functools.partial(exchange_kernel, FREE, PARTS),
        out_shape=[
            jax.ShapeDtypeStruct((4, 4) + blk, f32),
            jax.ShapeDtypeStruct((4, 4) + blk, f32),
            jax.ShapeDtypeStruct((4, 8) + blk, f32),
            jax.ShapeDtypeStruct((4, BS, 4 * BS), f32),
            jax.ShapeDtypeStruct((4, 2, 2) + blk, f32),
        ],
        in_specs=[smem, smem, any_, any_],
        out_specs=[any_] * 5,
        scratch_shapes=[
            V((4, BS, 4 * BS), f32), V((4, 2) + blk, f32),
            V((4,) + blk, f32), V((4,) + blk, f32), V((4,) + blk, f32), V((4,) + blk, f32),
            V((4, 4) + blk, f32), V((8,) + blk, f32), V((BS, 4 * BS), f32),
            V((8 * BS, BS), f32), V((BS, 4 * BS), f32),
            V((4,) + blk, f32), V((4,) + blk, f32), V((4,) + blk, f32), V((4,) + blk, f32),
            dma((4,)), dma((2,)), dma((4,)), dma((4,)), dma((4, 4)), dma((4, 4)), dma((4, 4)),
            dma((4, 4)), dma((4,)),
            dma((2, 4)), dma((2,)), dma((1,)), dma((2, 8)), dma((2, 8)), dma((2, 8)), dma((2, 8)),
            dma((2, 8)), dma((2, 8, 4)),
            dma((4, 2, 2)), dma((4, 2, 2)), dma((2, 2)), dma((1,)), dma((4, 2, 2)), dma((4, 2, 2)),
            dma((2, 2)), dma((2,)), dma((4,)), dma((4,)),
        ],
        compiler_params=pltpu.CompilerParams(
            collective_id=0, has_side_effects=True, vmem_limit_bytes=48 * 2**20
        ),
        name="exchange",
    )(index_map, fill_mask, contrib, front)

    Vh, Vl, frow = pl.pallas_call(
        panel_kernel,
        out_shape=[
            jax.ShapeDtypeStruct((4 * BS, 4 * BS), bf16),
            jax.ShapeDtypeStruct((4 * BS, 4 * BS), bf16),
            jax.ShapeDtypeStruct((BS, 4 * BS), f32),
        ],
        in_specs=[smem, vmem, vmem, vmem],
        out_specs=[vmem] * 3,
        scratch_shapes=[V((4 * BS, 4 * BS), f32), V((4 * BS, 4 * BS), f32)],
        compiler_params=pltpu.CompilerParams(vmem_limit_bytes=56 * 2**20),
        name="panel",
    )(pos, CR, UR, pivot_inverse)

    def child_spec(own):
        def index(l, imap, mask, pos):
            child = pos[1] // 8
            if not own:
                child = 1 - child
            return 0, child_row(imap, pos, child, l)[0], 0, 0

        return pl.BlockSpec((4, 1) + blk, index)

    return pl.pallas_call(
        update_kernel,
        out_shape=jax.ShapeDtypeStruct(front.shape, f32),
        grid_spec=pltpu.PrefetchScalarGridSpec(
            num_scalar_prefetch=3,
            grid=(8,),
            in_specs=[
                pl.BlockSpec((BS, 4 * BS), lambda l, *_: (l, 0)),
                pl.BlockSpec((4, 1) + blk, lambda l, *_: (0, l, 0, 0)),
                child_spec(True),
                child_spec(False),
                pl.BlockSpec((4 * BS, 4 * BS), lambda l, *_: (0, 0)),
                pl.BlockSpec((4 * BS, 4 * BS), lambda l, *_: (0, 0)),
                pl.BlockSpec((BS, 4 * BS), lambda l, *_: (0, 0)),
            ],
            out_specs=pl.BlockSpec((BS, 4 * BS), lambda l, *_: (l, 0)),
            scratch_shapes=[V((4,) + blk, f32), V((BS, 4 * BS), bf16), V((BS, 4 * BS), bf16)],
        ),
        compiler_params=pltpu.CompilerParams(vmem_limit_bytes=48 * 2**20),
        name="update",
    )(index_map, fill_mask, pos, front, LR, R, X, Vh, Vl, frow)


def solution(mesh):
    in_specs = (P("row", "col"), P("row", "col"), P(), P(), P())
    out_specs = P("row", "col")
    return jax.shard_map(body, mesh=mesh, in_specs=in_specs, out_specs=out_specs, check_vma=False)
```

```python
import functools

import jax
import jax.numpy as jnp
from jax import lax
from jax.experimental import pallas as pl
from jax.experimental.pallas import tpu as pltpu
from jax.sharding import PartitionSpec as P

BS = 256
K = 4
WINDOW = 8
MESH = pl.DeviceIdType.MESH
f32 = jnp.float32
bf16 = jnp.bfloat16


def place(imap, child, g, h, z, core):
    t = imap[child, 8 * g] - 8 * g
    first = (core + t) % 2
    start = (4 * g + (t + first) // 2) % 8
    m = (z + 8 - start) % 4
    half = ((start + m) % 8) // 4
    block = 8 * g + t + first + 2 * m
    return half == h, block // 16


def local_row(imap, child, jj, r):
    t = imap[child, 8 * jj] - 8 * jj
    return jj + (t + (r + 64 - t) % 8) // 8


def exchange_kernel(
    full, free, imap, mask, contrib, front, pinv_hbm,
    R, X, LR, Vh_out, Vl_out, frow_out,
    UR, CR, PB, U, pinv, Vh, Vl, frow, ldp, outs,
    cv, SP, M0, M1, M2, M3, S, PC, PR, FC, FR, RB, RC,
    ld, ldf, cs, cr, zs, zr, xs, xr, own,
    ldb, ldc, lcopy, Ls, Lr, Lxs, Lcs, Lcr, L3s,
    Us, Ur, Ups, ucopy, Cs, Cr, Cps, ccopy, Ccs, Ccr,
):
    M = [M0, M1, M2, M3]
    r = lax.axis_index("row")
    c = lax.axis_index("col")
    y, e = r // 2, r % 2
    h, z, core = c // 8, (c // 2) % 4, c % 2

    def dev(y_, e_, h_, z_, core_):
        return (2 * y_ + e_, 8 * h_ + 2 * z_ + core_)

    core_peer = dev(y, e, h, z, 1 - core)
    x_peer = dev(y, e, 1 - h, z, core)
    e_peer = dev(y, 1 - e, h, z, core)

    def z_peer(z_):
        return dev(y, e, h, z_, core)

    def y_peer(y_):
        return dev(y_, e, h, z, core)

    def remote(src, dst, ss, rs, to):
        return pltpu.make_async_remote_copy(
            src_ref=src, dst_ref=dst, send_sem=ss, recv_sem=rs, device_id=to, device_id_type=MESH
        )

    def load_c(jj):
        return pltpu.make_async_copy(contrib.at[pl.ds(jj * BS, BS)], cv.at[jj], ld.at[jj])

    for jj in range(4):
        load_c(jj).start()
    never = jnp.bool_(False)
    is_col_source = (h == 0) & (z < 2)
    is_row_source = r < 4
    load_pinv = pltpu.make_async_copy(pinv_hbm, pinv, ldp.at[0])
    load_pinv.start()
    load_fc = pltpu.make_async_copy(front.at[:, pl.ds(0, BS)], FC, ldf.at[0])
    load_fr = pltpu.make_async_copy(front.at[pl.ds(0, BS)], FR, ldf.at[1])

    @pl.when(is_col_source)
    def _():
        load_fc.start()

    @pl.when(is_row_source)
    def _():
        load_fr.start()

    barrier = pltpu.get_barrier_semaphore()
    peers = [core_peer, x_peer, e_peer]
    peers += [z_peer((z + d) % 4) for d in (1, 2, 3)]
    peers += [y_peer((y + d) % 4) for d in (1, 3)]
    for p in peers:
        pl.semaphore_signal(barrier, inc=1, device_id=p, device_id_type=MESH)
    pl.semaphore_wait(barrier, len(peers))

    t_own = imap[h, 8 * z] - 8 * z
    odd_mine = (core + t_own) % 2
    start_own = (4 * z + (t_own + odd_mine) // 2) % 8

    def core_copy(jj):
        return remote(SP.at[jj], M[jj].at[pl.ds(2 * core, 2)], cs.at[jj], cr.at[jj], core_peer)

    def z_copy(jj, d):
        to = (z + d) % 4
        return remote(S.at[jj, to], R.at[z, jj], zs.at[jj, d], zr.at[jj, z], z_peer(to))

    def z_wait(jj, g):
        remote(S.at[jj, 0], R.at[g, jj], zs.at[jj, 0], zr.at[jj, g], z_peer(g)).wait_recv()

    def own_copy(jj):
        return pltpu.make_async_copy(S.at[jj, z], R.at[z, jj], own.at[jj])

    def x_own(jj):
        return remote(S.at[jj, z], X.at[z, jj], xs.at[jj, z], xr.at[jj, z], x_peer)

    def x_copy(jj, g):
        return remote(R.at[g, jj], X.at[g, jj], xs.at[jj, g], xr.at[jj, g], x_peer)

    sends_x = h == 0 if full == 1 else h >= 0
    gets_x = h == 1 if full == 1 else h >= 0
    queue = []

    def cross(jj, g):
        mine = isinstance(g, int) and g == 0 and free
        group = (z + g) % 4 if free else g
        if len(queue) >= WINDOW:
            behind = queue[len(queue) - WINDOW]

            @pl.when(sends_x)
            def _():
                x_copy(*behind).wait_send()

        queue.append((jj, group))
        if mine:
            @pl.when(sends_x)
            def _():
                x_own(jj).start()

            return
        if free:
            z_wait(jj, group)

            @pl.when(sends_x)
            def _():
                x_copy(jj, group).start()

            return

        @pl.when(z != group)
        def _():
            if full == 1 and group == 0 and jj > 0:
                @pl.when(z != 1)
                def _():
                    z_wait(jj, group)
            else:
                z_wait(jj, group)

            @pl.when(sends_x)
            def _():
                x_copy(jj, group).start()

        @pl.when((z == group) & sends_x)
        def _():
            x_own(jj).start()

    def swap_cores():
        for jj in range(4):
            load_c(jj).wait()
            for i in range(2):
                even = cv[jj, :, 2 * i * BS:(2 * i + 1) * BS]
                odd = cv[jj, :, (2 * i + 1) * BS:(2 * i + 2) * BS]
                SP[jj, i] = jnp.where(odd_mine == 1, even, odd)
                M[jj][2 * core + i] = jnp.where(odd_mine == 1, odd, even)
            core_copy(jj).start()

    def arrange(jj):
        core_copy(jj).wait_recv()
        for to in range(4):
            S[jj, to] = M[jj][(to + 8 - start_own) % 4]
        own_copy(jj).start()

    def z_send(jj):
        for d in (1, 3, 2):
            z_copy(jj, d).start()

    def z_send_first(jj):
        @pl.when(z == 0)
        def _():
            z_copy(jj, 1).start()

    def z_send_rest(jj):
        @pl.when(z != 0)
        def _():
            z_copy(jj, 1).start()

        for d in (3, 2):
            z_copy(jj, d).start()

    def own_waits():
        for jj in range(4):
            own_copy(jj).wait()

    def y_next(way):
        return y_peer((y + (1 if way == 0 else 3)) % 4)

    def u_rows(way, q):
        return pl.ds(way * 128 + q * 64, 64)

    def u_copy(k, way, q, src):
        return remote(
            src, UR.at[k, u_rows(way, q)], Us.at[k, way, q], Ur.at[k, way, q], y_next(way)
        )

    def u_held(k, way, q):
        return UR.at[k, u_rows(way, q)]

    def u_partner(way, q):
        return remote(
            PR.at[u_rows(way, q)], UR.at[r, u_rows(way, q)],
            Ups.at[way, q], Ur.at[r, way, q], e_peer,
        )

    own_u = pltpu.make_async_copy(PR, UR.at[jnp.minimum(r, 3)], ucopy.at[0])

    def send_row_panel():
        own_u.start()
        for q in range(2):
            for way in range(2):
                u_partner(way, q).start()
                u_copy(r, way, q, PR.at[u_rows(way, q)]).start()

    other = 1 - full

    def load_rb(g):
        return pltpu.make_async_copy(R.at[g, 0], RB.at[g], ldb.at[g])

    def load_xb(g):
        return pltpu.make_async_copy(X.at[g, 0], RB.at[g], ldb.at[g])

    def make_row_panel():
        @pl.when(is_row_source)
        def _():
            @pl.when(h == other)
            def _():
                for g in range(4):
                    load_rb(g).start()

            @pl.when(h != other)
            def _():
                for g in range(4):
                    if g == 0 and other == 1:
                        @pl.when(jnp.logical_not(is_col_source))
                        def _():
                            x_copy(0, 0).wait_recv()
                    else:
                        x_copy(0, g).wait_recv()
                    load_xb(g).start()

            load_fr.wait()
            for g in range(4):
                load_rb(g).wait()
            row_in = local_row(imap, other, 0, r) == 0
            hit = [place(imap, other, g, h, z, core) for g in range(4)]
            for lc in range(4):
                weights = [
                    jnp.where(lands & row_in & (at == lc), 1.0, 0.0).astype(f32) for lands, at in hit
                ]
                present = mask[r, c + 16 * lc].astype(f32)

                @pl.loop(0, 4)
                def _(q):
                    rows = pl.ds(pl.multiple_of(q * 64, 64), 64)
                    total = FR[rows, lc * BS:(lc + 1) * BS]
                    for g in range(4):
                        total = total + weights[g] * RB[g, rows, :]
                    PR[rows, lc * BS:(lc + 1) * BS] = total * present
            send_row_panel()

    def make_row_panel_free():
        @pl.when(is_row_source)
        def _():
            load_fr.wait()
            for lc in range(4):
                PR[:, lc * BS:(lc + 1) * BS] = (
                    FR[:, lc * BS:(lc + 1) * BS] * mask[r, c + 16 * lc].astype(f32)
                )
            send_row_panel()

    panel = 2 * z + core

    def l_next(l):
        return z_peer((z + (1 if l % 2 == 0 else 3)) % 4)

    def l_copy(s, l, src):
        return remote(src, LR.at[2 * s + core, l], Ls.at[s, l], Lr.at[s, l], l_next(l))

    def l_wait(s, l):
        l_copy(s, l, LR.at[2 * s + core, l]).wait_recv()

    def l_x(s, l):
        return remote(
            LR.at[2 * s + core, l], LR.at[2 * s + core, l], Lxs.at[s, l], Lr.at[s, l], x_peer
        )

    def l_x_source(l):
        return remote(PC.at[l], LR.at[panel, l], Lxs.at[z, l], Lr.at[z, l], x_peer)

    def l_core(s, l):
        return remote(
            LR.at[2 * s + core, l], LR.at[2 * s + core, l], Lcs.at[s, l], Lcr.at[s, l], core_peer
        )

    def l_three(s, l, d):
        return remote(
            LR.at[2 * s + core, l], LR.at[2 * s + core, l],
            L3s.at[s, l, d], Lr.at[s, l], z_peer((z + d) % 4),
        )

    shift = [0, 0, 2, 2, 1, 3, 1, 3]
    own_l = pltpu.make_async_copy(PC, LR.at[jnp.minimum(panel, 3)], lcopy.at[0])

    def send_column_block(l, value):
        PC[l] = value
        l_copy(z, l, PC.at[l]).start()
        if shift[l] == 0:
            l_x_source(l).start()

    def make_column_panel():
        @pl.when(is_col_source)
        def _():
            if other == 1:
                for jj in range(4):
                    x_copy(jj, 0).wait_recv()

            child = pltpu.make_async_copy((R if other == 0 else X).at[0], RC, ldc.at[0])
            child.start()
            load_fc.wait()
            child.wait()
            lands, lc = place(imap, other, 0, h, z, core)
            rows_at = [local_row(imap, other, jj, r) for jj in range(4)]
            for l in range(8):
                present = mask[r + 8 * l, c].astype(f32)
                index = jnp.int32(0)
                found = jnp.int32(0)
                for jj in range(4):
                    here = (rows_at[jj] == l).astype(jnp.int32)
                    index = jnp.where(here > 0, jj, index)
                    found = found + here
                weight = jnp.where(lands & (lc == 0) & (found > 0), 1.0, 0.0).astype(f32)
                send_column_block(l, (FC[l * BS:(l + 1) * BS, :] + weight * RC[index]) * present)
            own_l.start()

    def make_column_panel_free():
        @pl.when(is_col_source)
        def _():
            load_fc.wait()
            for l in range(8):
                send_column_block(l, FC[l * BS:(l + 1) * BS, :] * mask[r + 8 * l, c].astype(f32))
            own_l.start()

    def own_l_wait():
        @pl.when(is_col_source)
        def _():
            own_l.wait()

    def column_ring(step):
        for i in range(4):
            if not 1 <= step - i <= 3:
                continue
            for way in range(2):
                l = 2 * i + way
                for s in range(2):
                    dist = (z + 4 - s) % 4 if way == 0 else (s + 4 - z) % 4

                    @pl.when(dist == step - i)
                    def _():
                        l_wait(s, l)
                        if step - i < 3:
                            l_copy(s, l, LR.at[2 * s + core, l]).start()
                        if shift[l] != 0:
                            @pl.when(z == (s + shift[l]) % 4)
                            def _():
                                l_x(s, l).start()

                        l_core(s, l).start()

    def column_spread(l):
        for s in range(2):
            @pl.when(z == (s + shift[l]) % 4)
            def _():
                l_wait(s, l)
                for d in (1, 3, 2):
                    l_three(s, l, d).start()
                l_core(s, l).start()

    def column_rest(l):
        for s in range(2):
            @pl.when(z != (s + shift[l]) % 4)
            def _():
                l_wait(s, l)
                l_core(s, l).start()

    def column_slot(slot):
        @pl.when(h == 0)
        def _():
            if slot == 1:
                own_l_wait()
                for l in range(8):
                    @pl.when(z < 2)
                    def _():
                        l_core(z, l).start()

            column_ring(slot)
            if slot == 3:
                corner_start()

        @pl.when(h == 1)
        def _():
            if slot == 1:
                column_spread(0)
                column_spread(1)
            if slot == 2:
                column_rest(0)
                corner_start()
            if slot == 3:
                column_rest(1)
            if slot == 4:
                for l in (2, 3, 4, 5):
                    column_spread(l)
            if slot == 5:
                column_spread(6)
                column_spread(7)
                for l in (2, 3, 4, 5):
                    column_rest(l)
            if slot == 6:
                column_rest(6)
                column_rest(7)

    def c_held(k, s, q):
        return CR.at[k, core, s, pl.ds(128 * q, 128)]

    def c_from(s, q):
        return LR.at[2 * s + core, 0, pl.ds(128 * q, 128)]

    def c_copy(k, s, q, src):
        return remote(src, c_held(k, s, q), Cs.at[k, s, q], Cr.at[k, s, q], y_next(s))

    def c_partner(s, q):
        return remote(c_from(s, q), c_held(r, s, q), Cps.at[s, q], Cr.at[r, s, q], e_peer)

    def c_own(s):
        return pltpu.make_async_copy(
            LR.at[2 * s + core, 0], CR.at[jnp.minimum(r, 3), core, s], ccopy.at[s]
        )

    def c_core(k):
        return remote(CR.at[k, core], CR.at[k, core], Ccs.at[k], Ccr.at[k], core_peer)

    def ring_dist(k, way):
        s = k // 2
        return (y + 4 - s) % 4 if way == 0 else (s + 4 - y) % 4

    def row_ring(step):
        for q in range(2):
            if not 0 <= step - q <= 3:
                continue
            for k in range(4):
                for way in range(2):
                    @pl.when((r != k) & (ring_dist(k, way) == step - q))
                    def _():
                        u_copy(k, way, q, u_held(k, way, q)).wait_recv()
                        if step - q < 3:
                            u_copy(k, way, q, u_held(k, way, q)).start()

    def corner_ring(step):
        for q in range(2):
            if not 0 <= step - q <= 3:
                continue
            for k in range(4):
                for s in range(2):
                    @pl.when((r != k) & (ring_dist(k, s) == step - q))
                    def _():
                        c_copy(k, s, q, c_held(k, s, q)).wait_recv()
                        if step - q < 3:
                            c_copy(k, s, q, c_held(k, s, q)).start()

    def corner_start():
        @pl.when(is_row_source)
        def _():
            for q in range(2):
                for s in range(2):
                    c_partner(s, q).start()
                    c_copy(r, s, q, c_from(s, q)).start()
            for s in range(2):
                c_own(s).start()

    def corner_swap():
        @pl.when(is_row_source)
        def _():
            for s in range(2):
                c_own(s).wait()

        for k in range(4):
            c_core(k).start()

    if free:
        todo = [(jj, d) for jj in range(4) for d in (1, 3, 2)]
        make_column_panel_free()
        swap_cores()
        arrange(0)
        z_send(0)
        cross(0, 0)
        make_row_panel_free()
        arrange(1)
        cross(1, 0)
        z_later = {1: 1, 2: 2, 3: 3}
    else:
        todo = [(0, g) for g in range(4)]
        if full == 0:
            todo += [(jj, 0) for jj in range(1, 4)]
        early = len(todo)
        todo += [(jj, g) for jj in range(1, 4) for g in range(4) if (jj, g) not in todo]
        swap_cores()
        arrange(0)
        z_send(0)
        for jj in range(1, 4):
            arrange(jj)
            z_send_first(jj)
        z_later = {2: 2, 3: 3} if full == 1 else {}
        for jj in range(1, 4):
            if jj not in z_later:
                z_send_rest(jj)
        for item in todo[:early]:
            cross(*item)
        todo = todo[early:]
        own_waits()
        if full == 1:
            @pl.when(z == 1)
            def _():
                for jj in range(1, 4):
                    z_wait(jj, 0)

        make_column_panel()
        make_row_panel()
    for slot in range(1, 7):
        column_slot(slot)
        for step in {4: (0,), 5: (1, 2), 6: (3, 4)}.get(slot, ()):
            corner_ring(step)
        if slot in z_later:
            (z_send if free else z_send_rest)(z_later[slot])
        if free and slot == 1:
            arrange(2)
            cross(2, 0)
            arrange(3)
            cross(3, 0)
        if free and slot == 2:
            own_waits()
        if slot > 1:
            for item in todo[:2]:
                cross(*item)
            todo = todo[2:]
            row_ring(slot - 2)
    corner_swap()
    for item in todo:
        cross(*item)

    @pl.when(is_row_source)
    def _():
        own_u.wait()

    for k in range(4):
        c_core(k).wait()
    load_pinv.wait()
    factor_panels(r, c, CR, UR, pinv, Vh, Vl, frow, PB, U)
    out_copies = [
        pltpu.make_async_copy(src, dst, outs.at[i])
        for i, (src, dst) in enumerate(((Vh, Vh_out), (Vl, Vl_out), (frow, frow_out)))
    ]
    for copy in out_copies:
        copy.start()

    for jj in range(4):
        core_copy(jj).wait_send()
        for d in (1, 2, 3):
            z_copy(jj, d).wait_send()

    @pl.when(sends_x)
    def _():
        for item in queue[len(queue) - WINDOW:]:
            x_copy(*item).wait_send()

    @pl.when(gets_x)
    def _():
        for g in range(4):
            for jj in range(4):
                done = never
                if not free and jj == 0:
                    done = is_row_source & (h != other)
                if not free and g == 0 and other == 1:
                    done = done | is_col_source

                @pl.when(jnp.logical_not(done))
                def _():
                    x_copy(jj, g).wait_recv()

    for copy in out_copies:
        copy.wait()

    @pl.when(is_row_source)
    def _():
        for q in range(2):
            for way in range(2):
                u_partner(way, q).wait_send()
                u_copy(r, way, q, PR.at[u_rows(way, q)]).wait_send()
                c_partner(way, q).wait_send()
                c_copy(r, way, q, c_from(way, q)).wait_send()
    for k in range(4):
        for way in range(2):
            dist = ring_dist(k, way)

            @pl.when((r != k) & (dist < 3))
            def _():
                for q in range(2):
                    u_copy(k, way, q, u_held(k, way, q)).wait_send()
                    c_copy(k, way, q, c_held(k, way, q)).wait_send()
    for s in range(2):
        for l in range(8):
            dist = (z + 4 - s) % 4 if l % 2 == 0 else (s + 4 - z) % 4
            cross_z = (s + shift[l]) % 4

            @pl.when(h == 0)
            def _():
                @pl.when(dist < 3)
                def _():
                    l_copy(s, l, LR.at[2 * s + core, l]).wait_send()

                @pl.when(z == cross_z)
                def _():
                    l_x(s, l).wait_send()

            @pl.when((h == 1) & (z == cross_z))
            def _():
                for d in (1, 3, 2):
                    l_three(s, l, d).wait_send()

            l_core(s, l).wait()


def split(a):
    hi = a.astype(bf16)
    return hi, (a - hi.astype(f32)).astype(bf16)


def dot3(a, b):
    ah, al = a
    bh, bl = b
    d = functools.partial(jnp.dot, preferred_element_type=f32)
    return d(ah, bh) + (d(ah, bl) + d(al, bh))


def factor_panels(r, c, CR, UR, pinv, Vh, Vl, frow, PB, U):
    for k in range(4):
        for j in range(4):
            PB[k * BS:(k + 1) * BS, j * BS:(j + 1) * BS] = CR[k, j % 2, j // 2]
        U[k * BS:(k + 1) * BS, :] = UR[k]
    for k in range(3):
        at, rest = k * BS, (k + 1) * BS
        lower = dot3(split(PB[rest:, at:rest]), split(pinv[k]))
        PB[rest:, at:rest] = lower
        low = split(lower)
        PB[rest:, rest:] = PB[rest:, rest:] - dot3(low, split(PB[at:rest, rest:]))
        U[rest:, :] = U[rest:, :] - dot3(low, split(U[at:rest, :]))

    @pl.when(r < 4)
    def _():
        rows = pl.ds(pl.multiple_of(r * BS, BS), BS)
        frow[...] = U[rows, :]

        @pl.when(c < 4)
        def _():
            frow[:, 0:BS] = PB[rows, pl.ds(pl.multiple_of(c * BS, BS), BS)]

    @pl.when(r >= 4)
    def _():
        frow[...] = jnp.zeros_like(frow)

    @pl.when(c < 4)
    def _():
        on = lax.broadcasted_iota(jnp.int32, (K * BS, BS), 0)
        across = lax.broadcasted_iota(jnp.int32, (K * BS, BS), 1)
        U[:, 0:BS] = jnp.where(on == across + c * BS, -1.0, 0.0).astype(f32)

    for m in range(3, -1, -1):
        at, rest = m * BS, (m + 1) * BS
        total = U[at:rest, :]
        if m < 3:
            total = total - dot3(split(PB[at:rest, rest:]), (Vh[rest:, :], Vl[rest:, :]))
        vh, vl = split(dot3(split(pinv[m]), split(total)))
        Vh[at:rest, :] = vh
        Vl[at:rest, :] = vl


def child_step(imap, pos, child, l):
    at = [local_row(imap, child, jj, pos[0]) for jj in range(4)]
    passed = sum((a <= l).astype(jnp.int32) for a in at)
    found = sum((a == l).astype(jnp.int32) for a in at)
    return jnp.clip(passed - 1, 0, 3), found


def update_kernel(imap, mask, pos, F, LRl, R, X, Vh, Vl, frow, out, ah, al):
    l = pl.program_id(0)
    r, c = pos[0], pos[1]
    h, z, core = c // 8, (c // 2) % 4, c % 2
    for p in range(4):
        hi, lo = split(LRl[p, 0])
        ah[:, p * BS:(p + 1) * BS] = hi
        al[:, p * BS:(p + 1) * BS] = lo
    children = []
    for child, source in ((h, R), (1 - h, X)):
        found = child_step(imap, pos, child, l)[1]
        children.append((source, found, [place(imap, child, g, h, z, core) for g in range(4)]))
    for lc in range(4):
        cols = slice(lc * BS, (lc + 1) * BS)
        total = F[:, cols]
        for source, found, places in children:
            group = jnp.int32(0)
            hit = jnp.int32(0)
            for g, (lands, at) in enumerate(places):
                here = (lands & (at == lc)).astype(jnp.int32) * found
                group = jnp.where(here > 0, g, group)
                hit = hit + here
            total = total + jnp.where(hit > 0, source[group, 0], 0.0)
        present = mask[r + 8 * l, c + 16 * lc].astype(f32)
        if lc == 0:
            present = present * (c >= 4).astype(f32)
        product = dot3((ah[...], al[...]), (Vh[:, cols], Vl[:, cols]))
        out[:, cols] = total * present - product

    @pl.when((l == 0) & (r < 4))
    def _():
        out[...] = frow[...]


def exchange(full, free, index_map, fill_mask, contrib, front, pivot_inverse):
    any_ = pl.BlockSpec(memory_space=pl.ANY)
    smem = pl.BlockSpec(memory_space=pltpu.SMEM)
    V = pltpu.VMEM
    dma = pltpu.SemaphoreType.DMA
    blk = (BS, BS)
    side = (4 * BS, 4 * BS)
    return pl.pallas_call(
        functools.partial(exchange_kernel, full, free),
        out_shape=[
            jax.ShapeDtypeStruct((4, 4) + blk, f32),
            jax.ShapeDtypeStruct((4, 4) + blk, f32),
            jax.ShapeDtypeStruct((4, 8) + blk, f32),
            jax.ShapeDtypeStruct(side, bf16),
            jax.ShapeDtypeStruct(side, bf16),
            jax.ShapeDtypeStruct((BS, 4 * BS), f32),
        ],
        in_specs=[smem, smem, any_, any_, any_],
        out_specs=[any_] * 6,
        scratch_shapes=[
            V((4, BS, 4 * BS), f32), V((4, 2, 2) + blk, f32), V(side, f32), V(side, f32),
            V((4,) + blk, f32), V(side, bf16), V(side, bf16), V((BS, 4 * BS), f32),
            dma((1,)), dma((3,)),
            V((4, BS, 4 * BS), f32), V((4, 2) + blk, f32),
            V((4,) + blk, f32), V((4,) + blk, f32), V((4,) + blk, f32), V((4,) + blk, f32),
            V((4, 4) + blk, f32), V((8,) + blk, f32), V((BS, 4 * BS), f32),
            V((8 * BS, BS), f32), V((BS, 4 * BS), f32),
            V((4,) + blk, f32), V((4,) + blk, f32),
            dma((4,)), dma((2,)), dma((4,)), dma((4,)), dma((4, 4)), dma((4, 4)), dma((4, 4)),
            dma((4, 4)), dma((4,)),
            dma((4,)), dma((1,)), dma((1,)), dma((2, 8)), dma((2, 8)), dma((2, 8)), dma((2, 8)),
            dma((2, 8)), dma((2, 8, 4)),
            dma((4, 2, 2)), dma((4, 2, 2)), dma((2, 2)), dma((1,)), dma((4, 2, 2)), dma((4, 2, 2)),
            dma((2, 2)), dma((2,)), dma((4,)), dma((4,)),
        ],
        compiler_params=pltpu.CompilerParams(
            collective_id=2 * full + int(free), has_side_effects=True, vmem_limit_bytes=60 * 2**20
        ),
        name="exchange_%d%d" % (full, free),
    )(index_map, fill_mask, contrib, front, pivot_inverse)


def body(front, contrib, pivot_inverse, index_map, fill_mask):
    pos = jnp.stack([lax.axis_index("row"), lax.axis_index("col")]).astype(jnp.int32)
    steps = index_map[:, ::8] - 16 * jnp.arange(4, dtype=jnp.int32)
    full = jnp.where(jnp.all(steps[0] == 8), 0, 1)
    free = index_map[1 - full, 0] >= 4
    R, X, LR, Vh, Vl, frow = lax.switch(
        2 * full + free.astype(jnp.int32),
        [functools.partial(exchange, f, e) for f in (0, 1) for e in (False, True)],
        index_map, fill_mask, contrib, front, pivot_inverse,
    )
    blk = (BS, BS)
    side = (4 * BS, 4 * BS)
    V = pltpu.VMEM

    def child_spec(own):
        def index(l, imap, mask, pos):
            child = pos[1] // 8
            if not own:
                child = 1 - child
            return 0, child_step(imap, pos, child, l)[0], 0, 0

        return pl.BlockSpec((4, 1) + blk, index)

    return pl.pallas_call(
        update_kernel,
        out_shape=jax.ShapeDtypeStruct(front.shape, f32),
        grid_spec=pltpu.PrefetchScalarGridSpec(
            num_scalar_prefetch=3,
            grid=(8,),
            in_specs=[
                pl.BlockSpec((BS, 4 * BS), lambda l, *_: (l, 0)),
                pl.BlockSpec((4, 1) + blk, lambda l, *_: (0, l, 0, 0)),
                child_spec(True),
                child_spec(False),
                pl.BlockSpec(side, lambda l, *_: (0, 0)),
                pl.BlockSpec(side, lambda l, *_: (0, 0)),
                pl.BlockSpec((BS, 4 * BS), lambda l, *_: (0, 0)),
            ],
            out_specs=pl.BlockSpec((BS, 4 * BS), lambda l, *_: (l, 0)),
            scratch_shapes=[V((BS, 4 * BS), bf16), V((BS, 4 * BS), bf16)],
        ),
        compiler_params=pltpu.CompilerParams(vmem_limit_bytes=60 * 2**20),
        name="update",
    )(index_map, fill_mask, pos, front, LR, R, X, Vh, Vl, frow)


def solution(mesh):
    in_specs = (P("row", "col"), P("row", "col"), P(), P(), P())
    out_specs = P("row", "col")
    return jax.shard_map(body, mesh=mesh, in_specs=in_specs, out_specs=out_specs, check_vma=False)
```

```python
import functools

import jax
import jax.numpy as jnp
from jax import lax
from jax.experimental import pallas as pl
from jax.experimental.pallas import tpu as pltpu
from jax.sharding import PartitionSpec as P

BS = 256
K = 4
WINDOW = 8
MESH = pl.DeviceIdType.MESH
f32 = jnp.float32
bf16 = jnp.bfloat16


def place(imap, child, g, h, z, core):
    t = imap[child, 8 * g] - 8 * g
    first = (core + t) % 2
    start = (4 * g + (t + first) // 2) % 8
    m = (z + 8 - start) % 4
    half = ((start + m) % 8) // 4
    block = 8 * g + t + first + 2 * m
    return half == h, block // 16


def local_row(imap, child, jj, r):
    t = imap[child, 8 * jj] - 8 * jj
    return jj + (t + (r + 64 - t) % 8) // 8


def exchange_kernel(
    free, imap, mask, contrib, front, pinv_hbm,
    R, X, LR, Vh_out, Vl_out, frow_out,
    UR, CR, PB, U, pinv, Vh, Vl, frow, ldp, outs,
    cv, SP, M0, M1, M2, M3, S, PC, PR, FC, FR, RB, RC,
    ld, ldf, cs, cr, zs, zr, xs, xr, own,
    ldb, ldc, lcopy, Ls, Lr, Lxs, Lcs, Lcr, L3s,
    Us, Ur, Ups, ucopy, Cs, Cr, Cps, ccopy, Ccs, Ccr,
):
    M = [M0, M1, M2, M3]
    r = lax.axis_index("row")
    c = lax.axis_index("col")
    y, e = r // 2, r % 2
    h, z, core = c // 8, (c // 2) % 4, c % 2

    def dev(y_, e_, h_, z_, core_):
        return (2 * y_ + e_, 8 * h_ + 2 * z_ + core_)

    core_peer = dev(y, e, h, z, 1 - core)
    x_peer = dev(y, e, 1 - h, z, core)
    e_peer = dev(y, 1 - e, h, z, core)

    def z_peer(z_):
        return dev(y, e, h, z_, core)

    def y_peer(y_):
        return dev(y_, e, h, z, core)

    def remote(src, dst, ss, rs, to):
        return pltpu.make_async_remote_copy(
            src_ref=src, dst_ref=dst, send_sem=ss, recv_sem=rs, device_id=to, device_id_type=MESH
        )

    def load_c(jj):
        return pltpu.make_async_copy(contrib.at[pl.ds(jj * BS, BS)], cv.at[jj], ld.at[jj])

    for jj in range(4):
        load_c(jj).start()
    never = jnp.bool_(False)
    is_col_source = (h == 0) & (z < 2)
    is_row_source = r < 4
    load_pinv = pltpu.make_async_copy(pinv_hbm, pinv, ldp.at[0])
    load_pinv.start()
    load_fc = pltpu.make_async_copy(front.at[:, pl.ds(0, BS)], FC, ldf.at[0])
    load_fr = pltpu.make_async_copy(front.at[pl.ds(0, BS)], FR, ldf.at[1])

    @pl.when(is_col_source)
    def _():
        load_fc.start()

    @pl.when(is_row_source)
    def _():
        load_fr.start()

    barrier = pltpu.get_barrier_semaphore()
    peers = [core_peer, x_peer, e_peer]
    peers += [z_peer((z + d) % 4) for d in (1, 2, 3)]
    peers += [y_peer((y + d) % 4) for d in (1, 3)]
    for p in peers:
        pl.semaphore_signal(barrier, inc=1, device_id=p, device_id_type=MESH)
    pl.semaphore_wait(barrier, len(peers))

    t_own = imap[h, 8 * z] - 8 * z
    odd_mine = (core + t_own) % 2
    start_own = (4 * z + (t_own + odd_mine) // 2) % 8

    def core_copy(jj):
        return remote(SP.at[jj], M[jj].at[pl.ds(2 * core, 2)], cs.at[jj], cr.at[jj], core_peer)

    def z_copy(jj, d):
        to = (z + d) % 4
        return remote(S.at[jj, to], R.at[z, jj], zs.at[jj, d], zr.at[jj, z], z_peer(to))

    def z_wait(jj, g):
        remote(S.at[jj, 0], R.at[g, jj], zs.at[jj, 0], zr.at[jj, g], z_peer(g)).wait_recv()

    def own_copy(jj):
        return pltpu.make_async_copy(S.at[jj, z], R.at[z, jj], own.at[jj])

    def x_own(jj):
        return remote(S.at[jj, z], X.at[z, jj], xs.at[jj, z], xr.at[jj, z], x_peer)

    def x_copy(jj, g):
        return remote(R.at[g, jj], X.at[g, jj], xs.at[jj, g], xr.at[jj, g], x_peer)

    queue = []

    def cross(jj, g):
        group = (z + g) % 4 if free else g
        if len(queue) >= WINDOW:
            x_copy(*queue[len(queue) - WINDOW]).wait_send()
        queue.append((jj, group))
        if free and g == 0:
            x_own(jj).start()
            return
        if free:
            z_wait(jj, group)
            x_copy(jj, group).start()
            return

        @pl.when(z != group)
        def _():
            z_wait(jj, group)
            x_copy(jj, group).start()

        @pl.when(z == group)
        def _():
            x_own(jj).start()

    def swap_cores():
        for jj in range(4):
            load_c(jj).wait()
            for i in range(2):
                even = cv[jj, :, 2 * i * BS:(2 * i + 1) * BS]
                odd = cv[jj, :, (2 * i + 1) * BS:(2 * i + 2) * BS]
                SP[jj, i] = jnp.where(odd_mine == 1, even, odd)
                M[jj][2 * core + i] = jnp.where(odd_mine == 1, odd, even)
            core_copy(jj).start()

    def arrange(jj):
        core_copy(jj).wait_recv()
        for to in range(4):
            S[jj, to] = M[jj][(to + 8 - start_own) % 4]
        own_copy(jj).start()

    def z_send(jj):
        for d in (1, 3, 2):
            z_copy(jj, d).start()

    def z_send_first(jj):
        @pl.when(z == 0)
        def _():
            z_copy(jj, 1).start()

    def z_send_rest(jj):
        @pl.when(z != 0)
        def _():
            z_copy(jj, 1).start()

        for d in (3, 2):
            z_copy(jj, d).start()

    def own_waits():
        for jj in range(4):
            own_copy(jj).wait()

    def y_next(way):
        return y_peer((y + (1 if way == 0 else 3)) % 4)

    def u_rows(way, q):
        return pl.ds(way * 128 + q * 64, 64)

    def u_copy(k, way, q, src):
        return remote(
            src, UR.at[k, u_rows(way, q)], Us.at[k, way, q], Ur.at[k, way, q], y_next(way)
        )

    def u_held(k, way, q):
        return UR.at[k, u_rows(way, q)]

    def u_partner(way, q):
        return remote(
            PR.at[u_rows(way, q)], UR.at[r, u_rows(way, q)],
            Ups.at[way, q], Ur.at[r, way, q], e_peer,
        )

    own_u = pltpu.make_async_copy(PR, UR.at[jnp.minimum(r, 3)], ucopy.at[0])

    def send_row_panel():
        own_u.start()
        for q in range(2):
            for way in range(2):
                u_partner(way, q).start()
                u_copy(r, way, q, PR.at[u_rows(way, q)]).start()

    def load_rb(w, g):
        return pltpu.make_async_copy((R, X)[w].at[g, 0], RB.at[w, g], ldb.at[w, g])

    def make_row_panel():
        @pl.when(is_row_source)
        def _():
            for g in range(4):
                load_rb(0, g).start()
            for g in range(4):
                if g == 0:
                    @pl.when(jnp.logical_not(is_col_source))
                    def _():
                        x_copy(0, 0).wait_recv()
                else:
                    x_copy(0, g).wait_recv()
                load_rb(1, g).start()
            load_fr.wait()
            for w in range(2):
                for g in range(4):
                    load_rb(w, g).wait()
            hit = []
            for w, child in enumerate((h, 1 - h)):
                row_in = local_row(imap, child, 0, r) == 0
                for g in range(4):
                    lands, at = place(imap, child, g, h, z, core)
                    hit.append((w, g, lands & row_in, at))
            for lc in range(4):
                weights = [
                    (w, g, jnp.where(ok & (at == lc), 1.0, 0.0).astype(f32)) for w, g, ok, at in hit
                ]
                present = mask[r, c + 16 * lc].astype(f32)

                @pl.loop(0, 8)
                def _(q):
                    rows = pl.ds(pl.multiple_of(q * 32, 32), 32)
                    total = FR[rows, lc * BS:(lc + 1) * BS]
                    for w, g, weight in weights:
                        total = total + weight * RB[w, g, rows, :]
                    PR[rows, lc * BS:(lc + 1) * BS] = total * present
            send_row_panel()

    def make_row_panel_free():
        @pl.when(is_row_source)
        def _():
            load_fr.wait()
            for lc in range(4):
                PR[:, lc * BS:(lc + 1) * BS] = (
                    FR[:, lc * BS:(lc + 1) * BS] * mask[r, c + 16 * lc].astype(f32)
                )
            send_row_panel()

    panel = 2 * z + core

    def l_next(l):
        return z_peer((z + (1 if l % 2 == 0 else 3)) % 4)

    def l_copy(s, l, src):
        return remote(src, LR.at[2 * s + core, l], Ls.at[s, l], Lr.at[s, l], l_next(l))

    def l_wait(s, l):
        l_copy(s, l, LR.at[2 * s + core, l]).wait_recv()

    def l_x(s, l):
        return remote(
            LR.at[2 * s + core, l], LR.at[2 * s + core, l], Lxs.at[s, l], Lr.at[s, l], x_peer
        )

    def l_x_source(l):
        return remote(PC.at[l], LR.at[panel, l], Lxs.at[z, l], Lr.at[z, l], x_peer)

    def l_core(s, l):
        return remote(
            LR.at[2 * s + core, l], LR.at[2 * s + core, l], Lcs.at[s, l], Lcr.at[s, l], core_peer
        )

    def l_three(s, l, d):
        return remote(
            LR.at[2 * s + core, l], LR.at[2 * s + core, l],
            L3s.at[s, l, d], Lr.at[s, l], z_peer((z + d) % 4),
        )

    shift = [0, 0, 2, 2, 1, 3, 1, 3]
    own_l = pltpu.make_async_copy(PC, LR.at[jnp.minimum(panel, 3)], lcopy.at[0])

    def send_column_block(l, value):
        PC[l] = value
        l_copy(z, l, PC.at[l]).start()
        if shift[l] == 0:
            l_x_source(l).start()

    def make_column_panel():
        @pl.when(is_col_source)
        def _():
            for jj in range(4):
                x_copy(jj, 0).wait_recv()
            loads = [pltpu.make_async_copy((R, X)[w].at[0], RC.at[w], ldc.at[w]) for w in range(2)]
            for load in loads:
                load.start()
            load_fc.wait()
            for load in loads:
                load.wait()
            hits = [place(imap, child, 0, h, z, core) for child in (h, 1 - h)]
            rows_at = [[local_row(imap, child, jj, r) for jj in range(4)] for child in (h, 1 - h)]
            for l in range(8):
                present = mask[r + 8 * l, c].astype(f32)
                total = FC[l * BS:(l + 1) * BS, :]
                for w in range(2):
                    lands, lc = hits[w]
                    index = jnp.int32(0)
                    found = jnp.int32(0)
                    for jj in range(4):
                        here = (rows_at[w][jj] == l).astype(jnp.int32)
                        index = jnp.where(here > 0, jj, index)
                        found = found + here
                    weight = jnp.where(lands & (lc == 0) & (found > 0), 1.0, 0.0).astype(f32)
                    total = total + weight * RC[w, index]
                send_column_block(l, total * present)
            own_l.start()

    def make_column_panel_free():
        @pl.when(is_col_source)
        def _():
            load_fc.wait()
            for l in range(8):
                send_column_block(l, FC[l * BS:(l + 1) * BS, :] * mask[r + 8 * l, c].astype(f32))
            own_l.start()

    def own_l_wait():
        @pl.when(is_col_source)
        def _():
            own_l.wait()

    def column_ring(step):
        for i in range(4):
            if not 1 <= step - i <= 3:
                continue
            for way in range(2):
                l = 2 * i + way
                for s in range(2):
                    dist = (z + 4 - s) % 4 if way == 0 else (s + 4 - z) % 4

                    @pl.when(dist == step - i)
                    def _():
                        l_wait(s, l)
                        if step - i < 3:
                            l_copy(s, l, LR.at[2 * s + core, l]).start()
                        if shift[l] != 0:
                            @pl.when(z == (s + shift[l]) % 4)
                            def _():
                                l_x(s, l).start()

                        l_core(s, l).start()

    def column_spread(l):
        for s in range(2):
            @pl.when(z == (s + shift[l]) % 4)
            def _():
                l_wait(s, l)
                for d in (1, 3, 2):
                    l_three(s, l, d).start()
                l_core(s, l).start()

    def column_rest(l):
        for s in range(2):
            @pl.when(z != (s + shift[l]) % 4)
            def _():
                l_wait(s, l)
                l_core(s, l).start()

    def column_slot(slot):
        @pl.when(h == 0)
        def _():
            if slot == 1:
                own_l_wait()
                for l in range(8):
                    @pl.when(z < 2)
                    def _():
                        l_core(z, l).start()

            column_ring(slot)
            if slot == 3:
                corner_start()

        @pl.when(h == 1)
        def _():
            if slot == 1:
                column_spread(0)
                column_spread(1)
            if slot == 2:
                column_rest(0)
                corner_start()
            if slot == 3:
                column_rest(1)
            if slot == 4:
                for l in (2, 3, 4, 5):
                    column_spread(l)
            if slot == 5:
                column_spread(6)
                column_spread(7)
                for l in (2, 3, 4, 5):
                    column_rest(l)
            if slot == 6:
                column_rest(6)
                column_rest(7)

    def c_held(k, s, q):
        return CR.at[k, core, s, pl.ds(128 * q, 128)]

    def c_from(s, q):
        return LR.at[2 * s + core, 0, pl.ds(128 * q, 128)]

    def c_copy(k, s, q, src):
        return remote(src, c_held(k, s, q), Cs.at[k, s, q], Cr.at[k, s, q], y_next(s))

    def c_partner(s, q):
        return remote(c_from(s, q), c_held(r, s, q), Cps.at[s, q], Cr.at[r, s, q], e_peer)

    def c_own(s):
        return pltpu.make_async_copy(
            LR.at[2 * s + core, 0], CR.at[jnp.minimum(r, 3), core, s], ccopy.at[s]
        )

    def c_core(k):
        return remote(CR.at[k, core], CR.at[k, core], Ccs.at[k], Ccr.at[k], core_peer)

    def ring_dist(k, way):
        s = k // 2
        return (y + 4 - s) % 4 if way == 0 else (s + 4 - y) % 4

    def row_ring(step):
        for q in range(2):
            if not 0 <= step - q <= 3:
                continue
            for k in range(4):
                for way in range(2):
                    @pl.when((r != k) & (ring_dist(k, way) == step - q))
                    def _():
                        u_copy(k, way, q, u_held(k, way, q)).wait_recv()
                        if step - q < 3:
                            u_copy(k, way, q, u_held(k, way, q)).start()

    def corner_ring(step):
        for q in range(2):
            if not 0 <= step - q <= 3:
                continue
            for k in range(4):
                for s in range(2):
                    @pl.when((r != k) & (ring_dist(k, s) == step - q))
                    def _():
                        c_copy(k, s, q, c_held(k, s, q)).wait_recv()
                        if step - q < 3:
                            c_copy(k, s, q, c_held(k, s, q)).start()

    def corner_start():
        @pl.when(is_row_source)
        def _():
            for q in range(2):
                for s in range(2):
                    c_partner(s, q).start()
                    c_copy(r, s, q, c_from(s, q)).start()
            for s in range(2):
                c_own(s).start()

    def corner_swap():
        @pl.when(is_row_source)
        def _():
            for s in range(2):
                c_own(s).wait()

        for k in range(4):
            c_core(k).start()

    if free:
        todo = [(jj, d) for jj in range(4) for d in (1, 3, 2)]
        make_column_panel_free()
        swap_cores()
        arrange(0)
        z_send(0)
        cross(0, 0)
        make_row_panel_free()
        arrange(1)
        cross(1, 0)
        z_later = {1: 1, 2: 2, 3: 3}
    else:
        todo = [(0, g) for g in range(4)] + [(jj, 0) for jj in range(1, 4)]
        todo += [(jj, g) for jj in range(1, 4) for g in range(1, 4)]
        swap_cores()
        arrange(0)
        z_send(0)
        for jj in range(1, 4):
            arrange(jj)
            z_send_first(jj)
        for jj in range(1, 4):
            z_send_rest(jj)
        for item in todo[:7]:
            cross(*item)
        todo = todo[7:]
        own_waits()
        make_column_panel()
        make_row_panel()
        z_later = {}
    for slot in range(1, 7):
        column_slot(slot)
        for step in {4: (0,), 5: (1, 2), 6: (3, 4)}.get(slot, ()):
            corner_ring(step)
        if slot in z_later:
            z_send(z_later[slot])
        if free and slot == 1:
            arrange(2)
            cross(2, 0)
            arrange(3)
            cross(3, 0)
        if free and slot == 2:
            own_waits()
        if slot > 1:
            for item in todo[:2]:
                cross(*item)
            todo = todo[2:]
            row_ring(slot - 2)
    corner_swap()
    for item in todo:
        cross(*item)

    @pl.when(is_row_source)
    def _():
        own_u.wait()

    for k in range(4):
        c_core(k).wait()
    load_pinv.wait()
    factor_panels(r, c, CR, UR, pinv, Vh, Vl, frow, PB, U)
    out_copies = [
        pltpu.make_async_copy(src, dst, outs.at[i])
        for i, (src, dst) in enumerate(((Vh, Vh_out), (Vl, Vl_out), (frow, frow_out)))
    ]
    for copy in out_copies:
        copy.start()

    for jj in range(4):
        core_copy(jj).wait_send()
        for d in (1, 2, 3):
            z_copy(jj, d).wait_send()

    for item in queue[len(queue) - WINDOW:]:
        x_copy(*item).wait_send()
    for g in range(4):
        for jj in range(4):
            done = never
            if not free and jj == 0:
                done = is_row_source
            if not free and g == 0:
                done = done | is_col_source

            @pl.when(jnp.logical_not(done))
            def _():
                x_copy(jj, g).wait_recv()

    for copy in out_copies:
        copy.wait()

    @pl.when(is_row_source)
    def _():
        for q in range(2):
            for way in range(2):
                u_partner(way, q).wait_send()
                u_copy(r, way, q, PR.at[u_rows(way, q)]).wait_send()
                c_partner(way, q).wait_send()
                c_copy(r, way, q, c_from(way, q)).wait_send()
    for k in range(4):
        for way in range(2):
            dist = ring_dist(k, way)

            @pl.when((r != k) & (dist < 3))
            def _():
                for q in range(2):
                    u_copy(k, way, q, u_held(k, way, q)).wait_send()
                    c_copy(k, way, q, c_held(k, way, q)).wait_send()
    for s in range(2):
        for l in range(8):
            dist = (z + 4 - s) % 4 if l % 2 == 0 else (s + 4 - z) % 4
            cross_z = (s + shift[l]) % 4

            @pl.when(h == 0)
            def _():
                @pl.when(dist < 3)
                def _():
                    l_copy(s, l, LR.at[2 * s + core, l]).wait_send()

                @pl.when(z == cross_z)
                def _():
                    l_x(s, l).wait_send()

            @pl.when((h == 1) & (z == cross_z))
            def _():
                for d in (1, 3, 2):
                    l_three(s, l, d).wait_send()

            l_core(s, l).wait()


def split(a):
    hi = a.astype(bf16)
    return hi, (a - hi.astype(f32)).astype(bf16)


def dot3(a, b):
    ah, al = a
    bh, bl = b
    d = functools.partial(jnp.dot, preferred_element_type=f32)
    return d(ah, bh) + (d(ah, bl) + d(al, bh))


def factor_panels(r, c, CR, UR, pinv, Vh, Vl, frow, PB, U):
    for k in range(4):
        for j in range(4):
            PB[k * BS:(k + 1) * BS, j * BS:(j + 1) * BS] = CR[k, j % 2, j // 2]
        U[k * BS:(k + 1) * BS, :] = UR[k]
    for k in range(3):
        at, rest = k * BS, (k + 1) * BS
        lower = dot3(split(PB[rest:, at:rest]), split(pinv[k]))
        PB[rest:, at:rest] = lower
        low = split(lower)
        PB[rest:, rest:] = PB[rest:, rest:] - dot3(low, split(PB[at:rest, rest:]))
        U[rest:, :] = U[rest:, :] - dot3(low, split(U[at:rest, :]))

    @pl.when(r < 4)
    def _():
        rows = pl.ds(pl.multiple_of(r * BS, BS), BS)
        frow[...] = U[rows, :]

        @pl.when(c < 4)
        def _():
            frow[:, 0:BS] = PB[rows, pl.ds(pl.multiple_of(c * BS, BS), BS)]

    @pl.when(r >= 4)
    def _():
        frow[...] = jnp.zeros_like(frow)

    @pl.when(c < 4)
    def _():
        on = lax.broadcasted_iota(jnp.int32, (K * BS, BS), 0)
        across = lax.broadcasted_iota(jnp.int32, (K * BS, BS), 1)
        U[:, 0:BS] = jnp.where(on == across + c * BS, -1.0, 0.0).astype(f32)

    for m in range(3, -1, -1):
        at, rest = m * BS, (m + 1) * BS
        total = U[at:rest, :]
        if m < 3:
            total = total - dot3(split(PB[at:rest, rest:]), (Vh[rest:, :], Vl[rest:, :]))
        vh, vl = split(dot3(split(pinv[m]), split(total)))
        Vh[at:rest, :] = vh
        Vl[at:rest, :] = vl


def child_step(imap, pos, child, l):
    at = [local_row(imap, child, jj, pos[0]) for jj in range(4)]
    passed = sum((a <= l).astype(jnp.int32) for a in at)
    found = sum((a == l).astype(jnp.int32) for a in at)
    return jnp.clip(passed - 1, 0, 3), found


def update_kernel(imap, mask, pos, F, LRl, R, X, Vh, Vl, frow, out, ah, al):
    l = pl.program_id(0)
    r, c = pos[0], pos[1]
    h, z, core = c // 8, (c // 2) % 4, c % 2
    for p in range(4):
        hi, lo = split(LRl[p, 0])
        ah[:, p * BS:(p + 1) * BS] = hi
        al[:, p * BS:(p + 1) * BS] = lo
    children = []
    for child, source in ((h, R), (1 - h, X)):
        found = child_step(imap, pos, child, l)[1]
        children.append((source, found, [place(imap, child, g, h, z, core) for g in range(4)]))
    for lc in range(4):
        cols = slice(lc * BS, (lc + 1) * BS)
        total = F[:, cols]
        for source, found, places in children:
            group = jnp.int32(0)
            hit = jnp.int32(0)
            for g, (lands, at) in enumerate(places):
                here = (lands & (at == lc)).astype(jnp.int32) * found
                group = jnp.where(here > 0, g, group)
                hit = hit + here
            total = total + jnp.where(hit > 0, source[group, 0], 0.0)
        present = mask[r + 8 * l, c + 16 * lc].astype(f32)
        if lc == 0:
            present = present * (c >= 4).astype(f32)
        product = dot3((ah[...], al[...]), (Vh[:, cols], Vl[:, cols]))
        out[:, cols] = total * present - product

    @pl.when((l == 0) & (r < 4))
    def _():
        out[...] = frow[...]


def exchange(free, index_map, fill_mask, contrib, front, pivot_inverse):
    any_ = pl.BlockSpec(memory_space=pl.ANY)
    smem = pl.BlockSpec(memory_space=pltpu.SMEM)
    V = pltpu.VMEM
    dma = pltpu.SemaphoreType.DMA
    blk = (BS, BS)
    side = (4 * BS, 4 * BS)
    return pl.pallas_call(
        functools.partial(exchange_kernel, free),
        out_shape=[
            jax.ShapeDtypeStruct((4, 4) + blk, f32),
            jax.ShapeDtypeStruct((4, 4) + blk, f32),
            jax.ShapeDtypeStruct((4, 8) + blk, f32),
            jax.ShapeDtypeStruct(side, bf16),
            jax.ShapeDtypeStruct(side, bf16),
            jax.ShapeDtypeStruct((BS, 4 * BS), f32),
        ],
        in_specs=[smem, smem, any_, any_, any_],
        out_specs=[any_] * 6,
        scratch_shapes=[
            V((4, BS, 4 * BS), f32), V((4, 2, 2) + blk, f32), V(side, f32), V(side, f32),
            V((4,) + blk, f32), V(side, bf16), V(side, bf16), V((BS, 4 * BS), f32),
            dma((1,)), dma((3,)),
            V((4, BS, 4 * BS), f32), V((4, 2) + blk, f32),
            V((4,) + blk, f32), V((4,) + blk, f32), V((4,) + blk, f32), V((4,) + blk, f32),
            V((4, 4) + blk, f32), V((8,) + blk, f32), V((BS, 4 * BS), f32),
            V((8 * BS, BS), f32), V((BS, 4 * BS), f32),
            V((2, 4) + blk, f32), V((2, 4) + blk, f32),
            dma((4,)), dma((2,)), dma((4,)), dma((4,)), dma((4, 4)), dma((4, 4)), dma((4, 4)),
            dma((4, 4)), dma((4,)),
            dma((2, 4)), dma((2,)), dma((1,)), dma((2, 8)), dma((2, 8)), dma((2, 8)), dma((2, 8)),
            dma((2, 8)), dma((2, 8, 4)),
            dma((4, 2, 2)), dma((4, 2, 2)), dma((2, 2)), dma((1,)), dma((4, 2, 2)), dma((4, 2, 2)),
            dma((2, 2)), dma((2,)), dma((4,)), dma((4,)),
        ],
        compiler_params=pltpu.CompilerParams(
            collective_id=int(free), has_side_effects=True, vmem_limit_bytes=60 * 2**20
        ),
        name="exchange_%d" % free,
    )(index_map, fill_mask, contrib, front, pivot_inverse)


def body(front, contrib, pivot_inverse, index_map, fill_mask):
    pos = jnp.stack([lax.axis_index("row"), lax.axis_index("col")]).astype(jnp.int32)
    R, X, LR, Vh, Vl, frow = lax.cond(
        jnp.min(index_map[:, 0]) >= 4,
        functools.partial(exchange, True), functools.partial(exchange, False),
        index_map, fill_mask, contrib, front, pivot_inverse,
    )
    blk = (BS, BS)
    side = (4 * BS, 4 * BS)
    V = pltpu.VMEM

    def child_spec(own):
        def index(l, imap, mask, pos):
            child = pos[1] // 8
            if not own:
                child = 1 - child
            return 0, child_step(imap, pos, child, l)[0], 0, 0

        return pl.BlockSpec((4, 1) + blk, index)

    return pl.pallas_call(
        update_kernel,
        out_shape=jax.ShapeDtypeStruct(front.shape, f32),
        grid_spec=pltpu.PrefetchScalarGridSpec(
            num_scalar_prefetch=3,
            grid=(8,),
            in_specs=[
                pl.BlockSpec((BS, 4 * BS), lambda l, *_: (l, 0)),
                pl.BlockSpec((4, 1) + blk, lambda l, *_: (0, l, 0, 0)),
                child_spec(True),
                child_spec(False),
                pl.BlockSpec(side, lambda l, *_: (0, 0)),
                pl.BlockSpec(side, lambda l, *_: (0, 0)),
                pl.BlockSpec((BS, 4 * BS), lambda l, *_: (0, 0)),
            ],
            out_specs=pl.BlockSpec((BS, 4 * BS), lambda l, *_: (l, 0)),
            scratch_shapes=[V((BS, 4 * BS), bf16), V((BS, 4 * BS), bf16)],
        ),
        compiler_params=pltpu.CompilerParams(vmem_limit_bytes=60 * 2**20),
        name="update",
    )(index_map, fill_mask, pos, front, LR, R, X, Vh, Vl, frow)


def solution(mesh):
    in_specs = (P("row", "col"), P("row", "col"), P(), P(), P())
    out_specs = P("row", "col")
    return jax.shard_map(body, mesh=mesh, in_specs=in_specs, out_specs=out_specs, check_vma=False)
```

```python
import functools

import jax
import jax.numpy as jnp
from jax import lax
from jax.experimental import pallas as pl
from jax.experimental.pallas import tpu as pltpu
from jax.sharding import PartitionSpec as P

BS = 256
K = 4
WINDOW = 8
MESH = pl.DeviceIdType.MESH
f32 = jnp.float32
bf16 = jnp.bfloat16


def place(imap, child, g, h, z, core):
    t = imap[child, 8 * g] - 8 * g
    first = (core + t) % 2
    start = (4 * g + (t + first) // 2) % 8
    m = (z + 8 - start) % 4
    half = ((start + m) % 8) // 4
    block = 8 * g + t + first + 2 * m
    return half == h, block // 16


def local_row(imap, child, jj, r):
    t = imap[child, 8 * jj] - 8 * jj
    return jj + (t + (r + 64 - t) % 8) // 8


def exchange_kernel(
    free, imap, mask, contrib, front, pinv_hbm,
    R, X, LR, Vh_out, Vl_out, frow_out,
    UR, CR, PB, U, pinv, Vh, Vl, frow, ldp, outs,
    cv, SP, M0, M1, M2, M3, S, PC, PR, FC, FR, RB, RC,
    ld, ldf, cs, cr, zs, zr, xs, xr, own,
    ldb, ldc, lcopy, Ls, Lr, Lxs, Lcs, Lcr, L3s,
    Us, Ur, Ups, ucopy, Cs, Cr, Cps, ccopy, Ccs, Ccr,
):
    M = [M0, M1, M2, M3]
    r = lax.axis_index("row")
    c = lax.axis_index("col")
    y, e = r // 2, r % 2
    h, z, core = c // 8, (c // 2) % 4, c % 2

    def dev(y_, e_, h_, z_, core_):
        return (2 * y_ + e_, 8 * h_ + 2 * z_ + core_)

    core_peer = dev(y, e, h, z, 1 - core)
    x_peer = dev(y, e, 1 - h, z, core)
    e_peer = dev(y, 1 - e, h, z, core)

    def z_peer(z_):
        return dev(y, e, h, z_, core)

    def y_peer(y_):
        return dev(y_, e, h, z, core)

    def remote(src, dst, ss, rs, to):
        return pltpu.make_async_remote_copy(
            src_ref=src, dst_ref=dst, send_sem=ss, recv_sem=rs, device_id=to, device_id_type=MESH
        )

    def load_c(jj):
        return pltpu.make_async_copy(contrib.at[pl.ds(jj * BS, BS)], cv.at[jj], ld.at[jj])

    for jj in range(4):
        load_c(jj).start()
    never = jnp.bool_(False)
    is_col_source = (h == 0) & (z < 2)
    is_row_source = r < 4
    load_pinv = pltpu.make_async_copy(pinv_hbm, pinv, ldp.at[0])
    load_pinv.start()
    load_fc = pltpu.make_async_copy(front.at[:, pl.ds(0, BS)], FC, ldf.at[0])
    load_fr = pltpu.make_async_copy(front.at[pl.ds(0, BS)], FR, ldf.at[1])

    @pl.when(is_col_source)
    def _():
        load_fc.start()

    @pl.when(is_row_source)
    def _():
        load_fr.start()

    barrier = pltpu.get_barrier_semaphore()
    peers = [core_peer, x_peer, e_peer]
    peers += [z_peer((z + d) % 4) for d in (1, 2, 3)]
    peers += [y_peer((y + d) % 4) for d in (1, 3)]
    for p in peers:
        pl.semaphore_signal(barrier, inc=1, device_id=p, device_id_type=MESH)
    pl.semaphore_wait(barrier, len(peers))

    t_own = imap[h, 8 * z] - 8 * z
    odd_mine = (core + t_own) % 2
    start_own = (4 * z + (t_own + odd_mine) // 2) % 8

    def core_copy(jj):
        return remote(SP.at[jj], M[jj].at[pl.ds(2 * core, 2)], cs.at[jj], cr.at[jj], core_peer)

    def z_copy(jj, d):
        to = (z + d) % 4
        return remote(S.at[jj, to], R.at[z, jj], zs.at[jj, d], zr.at[jj, z], z_peer(to))

    def z_wait(jj, g):
        remote(S.at[jj, 0], R.at[g, jj], zs.at[jj, 0], zr.at[jj, g], z_peer(g)).wait_recv()

    def own_copy(jj):
        return pltpu.make_async_copy(S.at[jj, z], R.at[z, jj], own.at[jj])

    def x_own(jj):
        return remote(S.at[jj, z], X.at[z, jj], xs.at[jj, z], xr.at[jj, z], x_peer)

    def x_copy(jj, g):
        return remote(R.at[g, jj], X.at[g, jj], xs.at[jj, g], xr.at[jj, g], x_peer)

    queue = []

    def cross(jj, g):
        group = (z + g) % 4 if free else g
        if len(queue) >= WINDOW:
            x_copy(*queue[len(queue) - WINDOW]).wait_send()
        queue.append((jj, group))
        if free and g == 0:
            x_own(jj).start()
            return
        if free:
            z_wait(jj, group)
            x_copy(jj, group).start()
            return

        @pl.when(z != group)
        def _():
            z_wait(jj, group)
            x_copy(jj, group).start()

        @pl.when(z == group)
        def _():
            x_own(jj).start()

    def swap_cores():
        for jj in range(4):
            load_c(jj).wait()
            for i in range(2):
                even = cv[jj, :, 2 * i * BS:(2 * i + 1) * BS]
                odd = cv[jj, :, (2 * i + 1) * BS:(2 * i + 2) * BS]
                SP[jj, i] = jnp.where(odd_mine == 1, even, odd)
                M[jj][2 * core + i] = jnp.where(odd_mine == 1, odd, even)
            core_copy(jj).start()

    def arrange(jj):
        core_copy(jj).wait_recv()
        for to in range(4):
            S[jj, to] = M[jj][(to + 8 - start_own) % 4]
        own_copy(jj).start()

    def z_send(jj):
        for d in (1, 3, 2):
            z_copy(jj, d).start()

    def z_send_first(jj):
        @pl.when(z == 0)
        def _():
            z_copy(jj, 1).start()

    def z_send_rest(jj):
        @pl.when(z != 0)
        def _():
            z_copy(jj, 1).start()

        for d in (3, 2):
            z_copy(jj, d).start()

    def own_waits():
        for jj in range(4):
            own_copy(jj).wait()

    def y_next(way):
        return y_peer((y + (1 if way == 0 else 3)) % 4)

    def u_rows(way, q):
        return pl.ds(way * 128 + q * 64, 64)

    def u_copy(k, way, q, src):
        return remote(
            src, UR.at[k, u_rows(way, q)], Us.at[k, way, q], Ur.at[k, way, q], y_next(way)
        )

    def u_held(k, way, q):
        return UR.at[k, u_rows(way, q)]

    def u_partner(way, q):
        return remote(
            PR.at[u_rows(way, q)], UR.at[r, u_rows(way, q)],
            Ups.at[way, q], Ur.at[r, way, q], e_peer,
        )

    own_u = pltpu.make_async_copy(PR, UR.at[jnp.minimum(r, 3)], ucopy.at[0])

    def send_row_panel():
        own_u.start()
        for q in range(2):
            for way in range(2):
                u_partner(way, q).start()
                u_copy(r, way, q, PR.at[u_rows(way, q)]).start()

    def load_rb(w, g):
        return pltpu.make_async_copy((R, X)[w].at[g, 0], RB.at[w, g], ldb.at[w, g])

    def make_row_panel():
        @pl.when(is_row_source)
        def _():
            for g in range(4):
                load_rb(0, g).start()
            for g in range(4):
                if g == 0:
                    @pl.when(jnp.logical_not(is_col_source))
                    def _():
                        x_copy(0, 0).wait_recv()
                else:
                    x_copy(0, g).wait_recv()
                load_rb(1, g).start()
            load_fr.wait()
            for w in range(2):
                for g in range(4):
                    load_rb(w, g).wait()
            hit = []
            for w, child in enumerate((h, 1 - h)):
                row_in = local_row(imap, child, 0, r) == 0
                for g in range(4):
                    lands, at = place(imap, child, g, h, z, core)
                    hit.append((w, g, lands & row_in, at))
            for lc in range(4):
                weights = [
                    (w, g, jnp.where(ok & (at == lc), 1.0, 0.0).astype(f32)) for w, g, ok, at in hit
                ]
                present = mask[r, c + 16 * lc].astype(f32)

                @pl.loop(0, 8)
                def _(q):
                    rows = pl.ds(pl.multiple_of(q * 32, 32), 32)
                    total = FR[rows, lc * BS:(lc + 1) * BS]
                    for w, g, weight in weights:
                        total = total + weight * RB[w, g, rows, :]
                    PR[rows, lc * BS:(lc + 1) * BS] = total * present
            send_row_panel()

    def make_row_panel_free():
        @pl.when(is_row_source)
        def _():
            load_fr.wait()
            for lc in range(4):
                PR[:, lc * BS:(lc + 1) * BS] = (
                    FR[:, lc * BS:(lc + 1) * BS] * mask[r, c + 16 * lc].astype(f32)
                )
            send_row_panel()

    panel = 2 * z + core

    def l_next(l):
        return z_peer((z + (1 if l % 2 == 0 else 3)) % 4)

    def l_copy(s, l, src):
        return remote(src, LR.at[2 * s + core, l], Ls.at[s, l], Lr.at[s, l], l_next(l))

    def l_wait(s, l):
        l_copy(s, l, LR.at[2 * s + core, l]).wait_recv()

    def l_x(s, l):
        return remote(
            LR.at[2 * s + core, l], LR.at[2 * s + core, l], Lxs.at[s, l], Lr.at[s, l], x_peer
        )

    def l_x_source(l):
        return remote(PC.at[l], LR.at[panel, l], Lxs.at[z, l], Lr.at[z, l], x_peer)

    def l_core(s, l):
        return remote(
            LR.at[2 * s + core, l], LR.at[2 * s + core, l], Lcs.at[s, l], Lcr.at[s, l], core_peer
        )

    def l_three(s, l, d):
        return remote(
            LR.at[2 * s + core, l], LR.at[2 * s + core, l],
            L3s.at[s, l, d], Lr.at[s, l], z_peer((z + d) % 4),
        )

    shift = [0, 0, 2, 2, 1, 3, 1, 3]
    own_l = pltpu.make_async_copy(PC, LR.at[jnp.minimum(panel, 3)], lcopy.at[0])

    def send_column_block(l, value):
        PC[l] = value
        l_copy(z, l, PC.at[l]).start()
        if shift[l] == 0:
            l_x_source(l).start()

    def make_column_panel():
        @pl.when(is_col_source)
        def _():
            for jj in range(4):
                x_copy(jj, 0).wait_recv()
            loads = [pltpu.make_async_copy((R, X)[w].at[0], RC.at[w], ldc.at[w]) for w in range(2)]
            for load in loads:
                load.start()
            load_fc.wait()
            for load in loads:
                load.wait()
            hits = [place(imap, child, 0, h, z, core) for child in (h, 1 - h)]
            rows_at = [[local_row(imap, child, jj, r) for jj in range(4)] for child in (h, 1 - h)]
            for l in range(8):
                present = mask[r + 8 * l, c].astype(f32)
                total = FC[l * BS:(l + 1) * BS, :]
                for w in range(2):
                    lands, lc = hits[w]
                    index = jnp.int32(0)
                    found = jnp.int32(0)
                    for jj in range(4):
                        here = (rows_at[w][jj] == l).astype(jnp.int32)
                        index = jnp.where(here > 0, jj, index)
                        found = found + here
                    weight = jnp.where(lands & (lc == 0) & (found > 0), 1.0, 0.0).astype(f32)
                    total = total + weight * RC[w, index]
                send_column_block(l, total * present)
            own_l.start()

    def make_column_panel_free():
        @pl.when(is_col_source)
        def _():
            load_fc.wait()
            for l in range(8):
                send_column_block(l, FC[l * BS:(l + 1) * BS, :] * mask[r + 8 * l, c].astype(f32))
            own_l.start()

    def own_l_wait():
        @pl.when(is_col_source)
        def _():
            own_l.wait()

    def column_ring(step):
        for i in range(4):
            if not 1 <= step - i <= 3:
                continue
            for way in range(2):
                l = 2 * i + way
                for s in range(2):
                    dist = (z + 4 - s) % 4 if way == 0 else (s + 4 - z) % 4

                    @pl.when(dist == step - i)
                    def _():
                        l_wait(s, l)
                        if step - i < 3:
                            l_copy(s, l, LR.at[2 * s + core, l]).start()
                        if shift[l] != 0:
                            @pl.when(z == (s + shift[l]) % 4)
                            def _():
                                l_x(s, l).start()

                        l_core(s, l).start()

    def column_spread(l):
        for s in range(2):
            @pl.when(z == (s + shift[l]) % 4)
            def _():
                l_wait(s, l)
                for d in (1, 3, 2):
                    l_three(s, l, d).start()
                l_core(s, l).start()

    def column_rest(l):
        for s in range(2):
            @pl.when(z != (s + shift[l]) % 4)
            def _():
                l_wait(s, l)
                l_core(s, l).start()

    def column_slot(slot):
        @pl.when(h == 0)
        def _():
            if slot == 1:
                own_l_wait()
                for l in range(8):
                    @pl.when(z < 2)
                    def _():
                        l_core(z, l).start()

            column_ring(slot)
            if slot == 3:
                corner_start()

        @pl.when(h == 1)
        def _():
            if slot == 1:
                column_spread(0)
                column_spread(1)
            if slot == 2:
                column_rest(0)
                corner_start()
            if slot == 3:
                column_rest(1)
            if slot == 4:
                for l in (2, 3, 4, 5):
                    column_spread(l)
            if slot == 5:
                column_spread(6)
                column_spread(7)
                for l in (2, 3, 4, 5):
                    column_rest(l)
            if slot == 6:
                column_rest(6)
                column_rest(7)

    def c_held(k, s, q):
        return CR.at[k, core, s, pl.ds(128 * q, 128)]

    def c_from(s, q):
        return LR.at[2 * s + core, 0, pl.ds(128 * q, 128)]

    def c_copy(k, s, q, src):
        return remote(src, c_held(k, s, q), Cs.at[k, s, q], Cr.at[k, s, q], y_next(s))

    def c_partner(s, q):
        return remote(c_from(s, q), c_held(r, s, q), Cps.at[s, q], Cr.at[r, s, q], e_peer)

    def c_own(s):
        return pltpu.make_async_copy(
            LR.at[2 * s + core, 0], CR.at[jnp.minimum(r, 3), core, s], ccopy.at[s]
        )

    def c_core(k, s, q):
        held = c_held(k, s, q)
        return remote(held, held, Ccs.at[k, s, q], Ccr.at[k, s, q], core_peer)

    def ring_dist(k, way):
        s = k // 2
        return (y + 4 - s) % 4 if way == 0 else (s + 4 - y) % 4

    def row_ring(step):
        for q in range(2):
            if not 0 <= step - q <= 3:
                continue
            for k in range(4):
                for way in range(2):
                    @pl.when((r != k) & (ring_dist(k, way) == step - q))
                    def _():
                        u_copy(k, way, q, u_held(k, way, q)).wait_recv()
                        if step - q < 3:
                            u_copy(k, way, q, u_held(k, way, q)).start()

    def corner_ring(step):
        for q in range(2):
            if not 0 <= step - q <= 3:
                continue
            for k in range(4):
                for s in range(2):
                    @pl.when((r != k) & (ring_dist(k, s) == step - q))
                    def _():
                        c_copy(k, s, q, c_held(k, s, q)).wait_recv()
                        if step - q < 3:
                            c_copy(k, s, q, c_held(k, s, q)).start()
                        c_core(k, s, q).start()

    def corner_start():
        @pl.when(is_row_source)
        def _():
            for q in range(2):
                for s in range(2):
                    c_partner(s, q).start()
                    c_copy(r, s, q, c_from(s, q)).start()
            for s in range(2):
                c_own(s).start()

    def corner_swap():
        @pl.when(is_row_source)
        def _():
            for s in range(2):
                c_own(s).wait()
                for q in range(2):
                    c_core(r, s, q).start()

    if free:
        todo = [(jj, d) for jj in range(4) for d in (1, 3, 2)]
        make_column_panel_free()
        swap_cores()
        arrange(0)
        z_send(0)
        cross(0, 0)
        make_row_panel_free()
        arrange(1)
        cross(1, 0)
        z_later = {1: 1, 2: 2, 3: 3}
    else:
        todo = [(0, g) for g in range(4)] + [(jj, 0) for jj in range(1, 4)]
        todo += [(jj, g) for jj in range(1, 4) for g in range(1, 4)]
        swap_cores()
        arrange(0)
        z_send(0)
        for jj in range(1, 4):
            arrange(jj)
            z_send_first(jj)
        for jj in range(1, 4):
            z_send_rest(jj)
        for item in todo[:7]:
            cross(*item)
        todo = todo[7:]
        own_waits()
        make_column_panel()
        make_row_panel()
        z_later = {}
    for slot in range(1, 7):
        column_slot(slot)
        for step in {4: (0,), 5: (1, 2), 6: (3, 4)}.get(slot, ()):
            corner_ring(step)
        if slot in z_later:
            z_send(z_later[slot])
        if free and slot == 1:
            arrange(2)
            cross(2, 0)
            arrange(3)
            cross(3, 0)
        if free and slot == 2:
            own_waits()
        if slot == 5:
            corner_swap()
        if slot > 1:
            for item in todo[:2]:
                cross(*item)
            todo = todo[2:]
            row_ring(slot - 2)
    for item in todo:
        cross(*item)

    @pl.when(is_row_source)
    def _():
        own_u.wait()

    for k in range(4):
        for s in range(2):
            for q in range(2):
                c_core(k, s, q).wait()
    load_pinv.wait()
    factor_panels(r, c, CR, UR, pinv, Vh, Vl, frow, PB, U)
    out_copies = [
        pltpu.make_async_copy(src, dst, outs.at[i])
        for i, (src, dst) in enumerate(((Vh, Vh_out), (Vl, Vl_out), (frow, frow_out)))
    ]
    for copy in out_copies:
        copy.start()

    for jj in range(4):
        core_copy(jj).wait_send()
        for d in (1, 2, 3):
            z_copy(jj, d).wait_send()

    for item in queue[len(queue) - WINDOW:]:
        x_copy(*item).wait_send()
    for g in range(4):
        for jj in range(4):
            done = never
            if not free and jj == 0:
                done = is_row_source
            if not free and g == 0:
                done = done | is_col_source

            @pl.when(jnp.logical_not(done))
            def _():
                x_copy(jj, g).wait_recv()

    for copy in out_copies:
        copy.wait()

    @pl.when(is_row_source)
    def _():
        for q in range(2):
            for way in range(2):
                u_partner(way, q).wait_send()
                u_copy(r, way, q, PR.at[u_rows(way, q)]).wait_send()
                c_partner(way, q).wait_send()
                c_copy(r, way, q, c_from(way, q)).wait_send()
    for k in range(4):
        for way in range(2):
            dist = ring_dist(k, way)

            @pl.when((r != k) & (dist < 3))
            def _():
                for q in range(2):
                    u_copy(k, way, q, u_held(k, way, q)).wait_send()
                    c_copy(k, way, q, c_held(k, way, q)).wait_send()
    for s in range(2):
        for l in range(8):
            dist = (z + 4 - s) % 4 if l % 2 == 0 else (s + 4 - z) % 4
            cross_z = (s + shift[l]) % 4

            @pl.when(h == 0)
            def _():
                @pl.when(dist < 3)
                def _():
                    l_copy(s, l, LR.at[2 * s + core, l]).wait_send()

                @pl.when(z == cross_z)
                def _():
                    l_x(s, l).wait_send()

            @pl.when((h == 1) & (z == cross_z))
            def _():
                for d in (1, 3, 2):
                    l_three(s, l, d).wait_send()

            l_core(s, l).wait()


def split(a):
    hi = a.astype(bf16)
    return hi, (a - hi.astype(f32)).astype(bf16)


def dot3(a, b):
    ah, al = a
    bh, bl = b
    d = functools.partial(jnp.dot, preferred_element_type=f32)
    return d(ah, bh) + (d(ah, bl) + d(al, bh))


def factor_panels(r, c, CR, UR, pinv, Vh, Vl, frow, PB, U):
    for k in range(4):
        for j in range(4):
            PB[k * BS:(k + 1) * BS, j * BS:(j + 1) * BS] = CR[k, j % 2, j // 2]
        U[k * BS:(k + 1) * BS, :] = UR[k]
    for k in range(3):
        at, rest = k * BS, (k + 1) * BS
        lower = dot3(split(PB[rest:, at:rest]), split(pinv[k]))
        PB[rest:, at:rest] = lower
        low = split(lower)
        PB[rest:, rest:] = PB[rest:, rest:] - dot3(low, split(PB[at:rest, rest:]))
        U[rest:, :] = U[rest:, :] - dot3(low, split(U[at:rest, :]))

    @pl.when(r < 4)
    def _():
        rows = pl.ds(pl.multiple_of(r * BS, BS), BS)
        frow[...] = U[rows, :]

        @pl.when(c < 4)
        def _():
            frow[:, 0:BS] = PB[rows, pl.ds(pl.multiple_of(c * BS, BS), BS)]

    @pl.when(r >= 4)
    def _():
        frow[...] = jnp.zeros_like(frow)

    @pl.when(c < 4)
    def _():
        on = lax.broadcasted_iota(jnp.int32, (K * BS, BS), 0)
        across = lax.broadcasted_iota(jnp.int32, (K * BS, BS), 1)
        U[:, 0:BS] = jnp.where(on == across + c * BS, -1.0, 0.0).astype(f32)

    for m in range(3, -1, -1):
        at, rest = m * BS, (m + 1) * BS
        total = U[at:rest, :]
        if m < 3:
            total = total - dot3(split(PB[at:rest, rest:]), (Vh[rest:, :], Vl[rest:, :]))
        vh, vl = split(dot3(split(pinv[m]), split(total)))
        Vh[at:rest, :] = vh
        Vl[at:rest, :] = vl


def child_step(imap, pos, child, l):
    at = [local_row(imap, child, jj, pos[0]) for jj in range(4)]
    passed = sum((a <= l).astype(jnp.int32) for a in at)
    found = sum((a == l).astype(jnp.int32) for a in at)
    return jnp.clip(passed - 1, 0, 3), found


def update_kernel(imap, mask, pos, F, LRl, R, X, Vh, Vl, frow, out, ah, al):
    l = pl.program_id(0)
    r, c = pos[0], pos[1]
    h, z, core = c // 8, (c // 2) % 4, c % 2
    for p in range(4):
        hi, lo = split(LRl[p, 0])
        ah[:, p * BS:(p + 1) * BS] = hi
        al[:, p * BS:(p + 1) * BS] = lo
    children = []
    for child, source in ((h, R), (1 - h, X)):
        found = child_step(imap, pos, child, l)[1]
        children.append((source, found, [place(imap, child, g, h, z, core) for g in range(4)]))
    for lc in range(4):
        cols = slice(lc * BS, (lc + 1) * BS)
        total = F[:, cols]
        for source, found, places in children:
            group = jnp.int32(0)
            hit = jnp.int32(0)
            for g, (lands, at) in enumerate(places):
                here = (lands & (at == lc)).astype(jnp.int32) * found
                group = jnp.where(here > 0, g, group)
                hit = hit + here
            total = total + jnp.where(hit > 0, source[group, 0], 0.0)
        present = mask[r + 8 * l, c + 16 * lc].astype(f32)
        if lc == 0:
            present = present * (c >= 4).astype(f32)
        product = dot3((ah[...], al[...]), (Vh[:, cols], Vl[:, cols]))
        out[:, cols] = total * present - product

    @pl.when((l == 0) & (r < 4))
    def _():
        out[...] = frow[...]


def exchange(free, index_map, fill_mask, contrib, front, pivot_inverse):
    any_ = pl.BlockSpec(memory_space=pl.ANY)
    smem = pl.BlockSpec(memory_space=pltpu.SMEM)
    V = pltpu.VMEM
    dma = pltpu.SemaphoreType.DMA
    blk = (BS, BS)
    side = (4 * BS, 4 * BS)
    return pl.pallas_call(
        functools.partial(exchange_kernel, free),
        out_shape=[
            jax.ShapeDtypeStruct((4, 4) + blk, f32),
            jax.ShapeDtypeStruct((4, 4) + blk, f32),
            jax.ShapeDtypeStruct((4, 8) + blk, f32),
            jax.ShapeDtypeStruct(side, bf16),
            jax.ShapeDtypeStruct(side, bf16),
            jax.ShapeDtypeStruct((BS, 4 * BS), f32),
        ],
        in_specs=[smem, smem, any_, any_, any_],
        out_specs=[any_] * 6,
        scratch_shapes=[
            V((4, BS, 4 * BS), f32), V((4, 2, 2) + blk, f32), V(side, f32), V(side, f32),
            V((4,) + blk, f32), V(side, bf16), V(side, bf16), V((BS, 4 * BS), f32),
            dma((1,)), dma((3,)),
            V((4, BS, 4 * BS), f32), V((4, 2) + blk, f32),
            V((4,) + blk, f32), V((4,) + blk, f32), V((4,) + blk, f32), V((4,) + blk, f32),
            V((4, 4) + blk, f32), V((8,) + blk, f32), V((BS, 4 * BS), f32),
            V((8 * BS, BS), f32), V((BS, 4 * BS), f32),
            V((2, 4) + blk, f32), V((2, 4) + blk, f32),
            dma((4,)), dma((2,)), dma((4,)), dma((4,)), dma((4, 4)), dma((4, 4)), dma((4, 4)),
            dma((4, 4)), dma((4,)),
            dma((2, 4)), dma((2,)), dma((1,)), dma((2, 8)), dma((2, 8)), dma((2, 8)), dma((2, 8)),
            dma((2, 8)), dma((2, 8, 4)),
            dma((4, 2, 2)), dma((4, 2, 2)), dma((2, 2)), dma((1,)), dma((4, 2, 2)), dma((4, 2, 2)),
            dma((2, 2)), dma((2,)), dma((4, 2, 2)), dma((4, 2, 2)),
        ],
        compiler_params=pltpu.CompilerParams(
            collective_id=int(free), has_side_effects=True, vmem_limit_bytes=60 * 2**20
        ),
        name="exchange_%d" % free,
    )(index_map, fill_mask, contrib, front, pivot_inverse)


def body(front, contrib, pivot_inverse, index_map, fill_mask):
    pos = jnp.stack([lax.axis_index("row"), lax.axis_index("col")]).astype(jnp.int32)
    R, X, LR, Vh, Vl, frow = lax.cond(
        jnp.min(index_map[:, 0]) >= 4,
        functools.partial(exchange, True), functools.partial(exchange, False),
        index_map, fill_mask, contrib, front, pivot_inverse,
    )
    blk = (BS, BS)
    side = (4 * BS, 4 * BS)
    V = pltpu.VMEM

    def child_spec(own):
        def index(l, imap, mask, pos):
            child = pos[1] // 8
            if not own:
                child = 1 - child
            return 0, child_step(imap, pos, child, l)[0], 0, 0

        return pl.BlockSpec((4, 1) + blk, index)

    return pl.pallas_call(
        update_kernel,
        out_shape=jax.ShapeDtypeStruct(front.shape, f32),
        grid_spec=pltpu.PrefetchScalarGridSpec(
            num_scalar_prefetch=3,
            grid=(8,),
            in_specs=[
                pl.BlockSpec((BS, 4 * BS), lambda l, *_: (l, 0)),
                pl.BlockSpec((4, 1) + blk, lambda l, *_: (0, l, 0, 0)),
                child_spec(True),
                child_spec(False),
                pl.BlockSpec(side, lambda l, *_: (0, 0)),
                pl.BlockSpec(side, lambda l, *_: (0, 0)),
                pl.BlockSpec((BS, 4 * BS), lambda l, *_: (0, 0)),
            ],
            out_specs=pl.BlockSpec((BS, 4 * BS), lambda l, *_: (l, 0)),
            scratch_shapes=[V((BS, 4 * BS), bf16), V((BS, 4 * BS), bf16)],
        ),
        compiler_params=pltpu.CompilerParams(vmem_limit_bytes=60 * 2**20),
        name="update",
    )(index_map, fill_mask, pos, front, LR, R, X, Vh, Vl, frow)


def solution(mesh):
    in_specs = (P("row", "col"), P("row", "col"), P(), P(), P())
    out_specs = P("row", "col")
    return jax.shard_map(body, mesh=mesh, in_specs=in_specs, out_specs=out_specs, check_vma=False)
```
